512 devices in a mesh: tm: 8 (over x, core), space: 64 (over y, z).
Axes of the slice: x: 4, y: 8, z: 8, core: 2. Of those that a mesh axis runs over, the one named last changes fastest.
Arguments:
- ensemble: bfloat16 [16, 131072, 256], P('tm', 'space'), may hold values from -6 to 6
- obs_index: int32 [16, 32768], P('tm', 'space'), may hold values from 0 to 2047
- obs_value: float32 [16, 32768], P('tm', 'space'), may hold values from -48 to 48
- obs_var: float32 [16, 32768], P('tm', 'space'), may hold values from 256 to 2048
Outputs:
- smoothed: bfloat16 [16, 131072, 256], P('tm', 'space')
The draws below stay inside these ranges and needn't reach their ends.
All inputs are finite; a program needn't handle non-finite values.
Results may differ from the reference program's by a relative error of at most 0.0049.
Values sent between devices are 32-bit elements; how exact they have to be, the bound alone decides.
A program may use at most 64 MiB of HBM per device.

```python
import math
import jax
import jax.numpy as jnp
from jax import lax

M = 256
ROWS_DEV = 2048
OBS_DEV = 512
NS_ITERS = 6
WINDOWS = 16
ROWS = 131072
OBS = 32768


def touch_ends(entries, rng, smallest, top_value):
    spot = [jax.random.randint(jax.random.fold_in(rng, axis), (), 0, length) for axis, length in enumerate(entries.shape)]
    longest = entries.shape.index(max(entries.shape))
    neighbour = spot[:longest] + [(spot[longest] + 1) % entries.shape[longest]] + spot[longest + 1:]
    return entries.at[tuple(spot)].set(smallest).at[tuple(neighbour)].set(top_value)


def steps_of(key, dims, shards, low, largest):
    def one(axis_at, parts):
        draws = jax.random.uniform(jax.random.fold_in(jax.random.fold_in(key, 6), axis_at), (parts,), jnp.float32, low / len(shards), largest / len(shards))
        return jnp.repeat(jnp.exp(draws), dims[axis_at] // parts).reshape((-1,) + (1,) * (len(dims) - axis_at - 1))

    factor_of = one(*shards[0])
    for cut in shards[1:]:
        factor_of = factor_of * one(*cut)
    return factor_of


def scatter_about(own_key, shape, scale, reach, split=(), held_as=jnp.bfloat16):
    entries = jax.random.normal(own_key, shape, jnp.float32) * scale
    if len(split) > 0:
        entries = steps_of(own_key, shape, split, -0.22, 0.18) * entries
    return jnp.clip(entries, min=-reach, max=reach).astype(held_as)


def setup_inputs(seed: int = 0) -> dict:
    seeds = jax.random.split(jax.random.key(seed), 5)
    ensemble = scatter_about(seeds[0], (WINDOWS, ROWS, M), 1.0, 6.0, ((0, 8), (1, 64)))
    obs_index = touch_ends(jax.random.randint(seeds[1], (WINDOWS, OBS), 0, ROWS_DEV), jax.random.fold_in(seeds[1], 1), 0, ROWS_DEV - 1).astype(jnp.int32)
    obs_value = scatter_about(seeds[2], (WINDOWS, OBS), 8.0, 48.0, ((0, 8), (1, 64)), jnp.float32)
    obs_var = jnp.clip(jnp.exp(math.log(2048.0) - 2.0794415 * jax.random.uniform(seeds[3], (WINDOWS, OBS), jnp.float32) ** steps_of(seeds[3], (WINDOWS, OBS), ((0, 8), (1, 64)), -0.2, 0.2)), 256.0, 2048.0)
    return dict(ensemble=ensemble, obs_index=obs_index, obs_value=obs_value, obs_var=obs_var)


HIGH = lax.Precision.HIGHEST

def window_transform(rows, value, var):
    mean = lax.optimization_barrier(jnp.mean(rows, axis=1, keepdims=True))
    anom = rows - mean
    innov = value - mean[:, 0]
    inv_var = 1.0 / var
    gram = jnp.dot(anom.T, anom * inv_var[:, None], precision=HIGH)
    proj = jnp.dot(innov * inv_var, anom, precision=HIGH)
    eye = jnp.eye(M, dtype=jnp.float32)
    amat = (M - 1.0) * eye + gram
    scale = jnp.sqrt(jnp.sum(amat * amat))
    ycur = amat / scale
    zcur = eye
    for step in range(NS_ITERS):
        tmat = 1.5 * eye - 0.5 * jnp.dot(zcur, ycur, precision=HIGH)
        ycur = jnp.dot(ycur, tmat, precision=HIGH)
        zcur = jnp.dot(tmat, zcur, precision=HIGH)
    wmean = jnp.dot(zcur, jnp.dot(zcur, proj, precision=HIGH), precision=HIGH) / scale
    wtrans = jnp.sqrt(M - 1.0) * zcur / jnp.sqrt(scale)
    qmat = wmean[:, None] + wtrans
    return qmat - lax.optimization_barrier(jnp.mean(qmat, axis=0, keepdims=True)) + 1.0 / M

def reference(ensemble, obs_index, obs_value, obs_var):
    block = (jnp.arange(OBS) // OBS_DEV).astype(jnp.int32)
    gmats = []
    for w in range(WINDOWS):
        rows_at = (block * ROWS_DEV + obs_index[w]).astype(jnp.int32)
        rows = ensemble[w][rows_at].astype(jnp.float32)
        gmats.append(window_transform(rows, obs_value[w], obs_var[w]))
    results = [None] * WINDOWS
    suffix = jnp.eye(M, dtype=jnp.float32)
    for w in range(WINDOWS - 1, -1, -1):
        suffix = jnp.dot(gmats[w], suffix, precision=HIGH)
        results[w] = jnp.dot(ensemble[w], suffix.astype(jnp.bfloat16), preferred_element_type=jnp.float32).astype(jnp.bfloat16)
    return jnp.stack(results)
```

```python
import jax
import jax.numpy as jnp
from jax import lax
from jax.experimental import pallas as pl
from jax.experimental.pallas import tpu as pltpu
from jax.sharding import PartitionSpec as P

NS_ITERS = 6
M = 256
MESH = pl.DeviceIdType.MESH
F32 = jnp.float32
BF16 = jnp.bfloat16
ORDER = (4, 3, 5, 2, 6, 1, 7)
SHARD = 32
SENT = 40
VMEM_LIMIT = 40 * 2**20


def dot(a, b):
    return jnp.dot(a, b, preferred_element_type=F32)


def dot_nt(a, b):
    return lax.dot_general(a, b, (((1,), (1,)), ((), ())), preferred_element_type=F32)


def dot_tn(a, b):
    return lax.dot_general(a, b, (((0,), (0,)), ((), ())), preferred_element_type=F32)


def split(a):
    high = a.astype(BF16)
    return high, (a - high.astype(F32)).astype(BF16)


def dot3(a, b):
    left = jnp.concatenate([a[0], a[1], a[0]], axis=1)
    right = jnp.concatenate([b[0], b[0], b[1]], axis=0)
    return dot(left, right)


def local_sums(ens, index, value, var):
    inv = 1.0 / var
    low = index & 127
    high = index >> 7
    count = index.shape[1]
    at_low = jnp.where(lax.broadcasted_iota(jnp.int32, (128, count), 0) == low, 1.0, 0.0).astype(BF16)
    at_high = lax.broadcasted_iota(jnp.int32, (16, count), 0) == high
    terms = jnp.concatenate([jnp.where(at_high, inv, 0.0), jnp.where(at_high, value * inv, 0.0)], axis=0)
    first = terms.astype(BF16)
    rest = terms - first.astype(F32)
    second = rest.astype(BF16)
    third = (rest - second.astype(F32)).astype(BF16)
    columns = dot_nt(at_low, first) + (dot_nt(at_low, second) + dot_nt(at_low, third))
    rows = dot_nt(first, at_low) + (dot_nt(second, at_low) + dot_nt(third, at_low))
    s_row = jnp.concatenate([rows[16 + i : 17 + i, :] for i in range(16)], axis=1)
    s_first, s_second = split(s_row)
    s_both = jnp.concatenate([s_first, s_second, jnp.zeros((14, s_row.shape[1]), BF16)], axis=0)
    scaled = [split(ens[128 * i : 128 * (i + 1), :].astype(F32) * columns[:, i : i + 1]) for i in range(16)]
    scaled_first = jnp.concatenate([a for a, _ in scaled], axis=0)
    scaled_second = jnp.concatenate([b for _, b in scaled], axis=0)
    gram = dot_tn(ens, scaled_first) + dot_tn(ens, scaled_second)
    proj = dot(s_both, ens)
    return gram, proj[0:1, :] + proj[1:2, :]


def pack(gram, proj):
    r = lax.broadcasted_iota(jnp.int32, (128, 128), 0)
    c = lax.broadcasted_iota(jnp.int32, (128, 128), 1)
    k11, k12, k22 = gram[:128, :128], gram[:128, 128:], gram[128:, 128:]
    mixed = jnp.where(r >= c, k11, k22)
    diag = jnp.sum(jnp.where(r == c, k22, 0.0), axis=0, keepdims=True)
    extra = jnp.concatenate([diag, proj[:, :128], proj[:, 128:], jnp.zeros((5, 128), F32)], axis=0)
    return jnp.concatenate([k12, mixed], axis=0), extra


def unpack(body, extra):
    r = lax.broadcasted_iota(jnp.int32, (128, 128), 0)
    c = lax.broadcasted_iota(jnp.int32, (128, 128), 1)
    k12, mixed = body[:128, :], body[128:, :]
    turned = mixed.T
    k11 = jnp.where(r >= c, mixed, turned)
    k22 = jnp.where(r < c, mixed, jnp.where(r == c, extra[0:1, :], turned))
    gram = jnp.concatenate(
        [jnp.concatenate([k11, k12], axis=1), jnp.concatenate([k12.T, k22], axis=1)], axis=0
    )
    return gram, jnp.concatenate([extra[1:2, :], extra[2:3, :]], axis=1)


def transforms(sums):
    r = lax.broadcasted_iota(jnp.int32, (M, M), 0)
    c = lax.broadcasted_iota(jnp.int32, (M, M), 1)
    eye = jnp.where(r == c, 1.0, 0.0).astype(F32)
    count = range(len(sums))
    scales, projs, y, z = [], [], [], []
    for gram, proj in sums:
        col_mean = jnp.mean(gram, axis=0, keepdims=True)
        row_mean = jnp.mean(gram, axis=1, keepdims=True)
        amat = gram - row_mean - (col_mean - jnp.mean(col_mean, axis=1, keepdims=True)) + (M - 1.0) * eye
        scale = jnp.sqrt(jnp.sum(jnp.sum(amat * amat, axis=0, keepdims=True), axis=1, keepdims=True))
        start = amat / scale
        proj = proj - col_mean
        projs.append(proj - jnp.mean(proj, axis=1, keepdims=True))
        scales.append(scale)
        y.append(split(start))
        z.append(split(1.5 * eye - 0.5 * start))
    y = [split(dot3(y[w], z[w])) for w in count]
    for step in range(1, NS_ITERS):
        t = [split(1.5 * eye - 0.5 * dot3(z[w], y[w])) for w in count]
        last = [dot3(t[w], z[w]) for w in count]
        z = [split(last[w]) for w in count]
        if step < NS_ITERS - 1:
            y = [split(dot3(y[w], t[w])) for w in count]
    gmats = []
    for w in count:
        vec = dot3(split(jnp.broadcast_to(projs[w], (16, M))), z[w])
        vec = split(vec)
        mean = dot_nt(z[w][0], vec[0]) + (dot_nt(z[w][0], vec[1]) + dot_nt(z[w][1], vec[0]))
        wmean = mean[:, 0:1] / scales[w]
        wmean = wmean - jnp.mean(wmean, axis=0, keepdims=True)
        wtrans = last[w] * (jnp.sqrt(M - 1.0) / jnp.sqrt(scales[w]))
        gmats.append(wmean + (wtrans - jnp.mean(wtrans, axis=0, keepdims=True) + 1.0 / M))
    return gmats


def suffix_kernel(
    ens_ref, index_ref, value_ref, var_ref, out_ref,
    parts, got1, mine, got2, whole, extras, pair, half, chips, later,
    send1, recv1, send2, recv2, send3, recv3, core_send, core_recv, x_send, x_recv, f_send, f_recv,
):
    t = lax.axis_index("tm")
    s = lax.axis_index("space")
    x, core = t // 2, t % 2
    at = (s // 8, s % 8)

    def along(axis, by):
        spot = list(at)
        spot[axis] = (at[axis] + by) % 8
        return {"tm": t, "space": spot[0] * 8 + spot[1]}

    def on_x(by):
        return {"tm": ((x + by + 4) % 4) * 2 + core, "space": s}

    sibling = {"tm": x * 2 + 1 - core, "space": s}

    barrier = pltpu.get_barrier_semaphore()
    for by in ORDER:
        for axis in range(2):
            pl.semaphore_signal(barrier, inc=1, device_id=along(axis, by), device_id_type=MESH)
    for by in (1, 2, 3):
        pl.semaphore_signal(barrier, inc=1, device_id=on_x(by), device_id_type=MESH)
    pl.semaphore_signal(barrier, inc=1, device_id=sibling, device_id_type=MESH)

    def copy1(w, i):
        by = ORDER[i]
        return pltpu.make_async_remote_copy(
            src_ref=parts.at[w, (at[w] + by) % 8], dst_ref=got1.at[w, i], send_sem=send1.at[w, i],
            recv_sem=recv1.at[w, i], device_id=along(w, by), device_id_type=MESH,
        )

    def copy2(w, i):
        return pltpu.make_async_remote_copy(
            src_ref=mine.at[w], dst_ref=got2.at[w, i], send_sem=send2.at[w, i],
            recv_sem=recv2.at[w, i], device_id=along(1 - w, ORDER[i]), device_id_type=MESH,
        )

    def copy3(w, i):
        return pltpu.make_async_remote_copy(
            src_ref=whole.at[w, at[w]], dst_ref=whole.at[w, at[w]], send_sem=send3.at[w, i],
            recv_sem=recv3.at[w, i], device_id=along(w, ORDER[i]), device_id_type=MESH,
        )

    for w in range(2):
        gram, proj = local_sums(ens_ref[w], index_ref[w : w + 1, :], value_ref[w : w + 1, :], var_ref[w : w + 1, :])
        body, extra = pack(gram, proj)
        for k in range(8):
            parts[w, k, 0:SHARD, :] = body[SHARD * k : SHARD * (k + 1), :]
            parts[w, k, SHARD:SENT, :] = extra
        if w == 0:
            pl.semaphore_wait(barrier, 18)
        for i in range(7):
            copy1(w, i).start()

    for w in range(2):
        total = parts[w, at[w]]
        for i in range(7):
            copy1(w, i).wait_recv()
            total = total + got1[w, i]
        mine[w] = total
        for i in range(7):
            copy2(w, i).start()

    for w in range(2):
        total = mine[w]
        for i in range(7):
            copy2(w, i).wait_recv()
            total = total + got2[w, i]
        whole[w, at[w]] = total[:SHARD]
        extras[w] = total[SHARD:]
        for i in range(7):
            copy3(w, i).start()

    for w in range(2):
        for i in range(7):
            copy1(w, i).wait_send()
            copy2(w, i).wait_send()
    for w in range(2):
        for i in range(7):
            copy3(w, i).wait_recv()

    g0, g1 = transforms([unpack(whole[w].reshape(256, 128), extras[w]) for w in range(2)])
    g0, g1 = split(g0), split(g1)
    own = dot3(g0, g1)
    pair[core] = own
    swap = pltpu.make_async_remote_copy(
        src_ref=pair.at[core], dst_ref=pair.at[core], send_sem=core_send, recv_sem=core_recv,
        device_id=sibling, device_id_type=MESH,
    )
    swap.start()
    r = lax.broadcasted_iota(jnp.int32, (128, M), 0)
    c = lax.broadcasted_iota(jnp.int32, (128, M), 1)
    for j in range(3):
        @pl.when(j < x)
        def _():
            for h in range(2):
                chips[j, h] = jnp.where(r + 128 * h == c, 1.0, 0.0).astype(F32)
    swap.wait()
    odd = split(pair[1])
    half[...] = dot3(split(pair[0, pl.ds(pl.multiple_of(core * 128, 128), 128), :]), odd)

    def copy_x(by):
        return pltpu.make_async_remote_copy(
            src_ref=half, dst_ref=chips.at[x - 1, core], send_sem=x_send.at[by - 1], recv_sem=x_recv.at[x - 1],
            device_id=on_x(-by), device_id_type=MESH,
        )

    def arrived(j):
        return pltpu.make_async_remote_copy(
            src_ref=half, dst_ref=chips.at[j, core], send_sem=x_send.at[0], recv_sem=x_recv.at[j],
            device_id=sibling, device_id_type=MESH,
        )

    def pass_on(j):
        return pltpu.make_async_remote_copy(
            src_ref=chips.at[j, core], dst_ref=chips.at[j, core], send_sem=f_send.at[j], recv_sem=f_recv.at[j],
            device_id=sibling, device_id_type=MESH,
        )

    def passed(j):
        return pltpu.make_async_remote_copy(
            src_ref=chips.at[j, core], dst_ref=chips.at[j, 1 - core], send_sem=f_send.at[j], recv_sem=f_recv.at[j],
            device_id=sibling, device_id_type=MESH,
        )

    for by in (1, 2, 3):
        @pl.when(x >= by)
        def _():
            copy_x(by).start()
    for j in range(3):
        @pl.when(x <= j)
        def _():
            arrived(j).wait_recv()
            pass_on(j).start()
    for j in range(3):
        @pl.when(x <= j)
        def _():
            passed(j).wait_recv()
    for w in range(2):
        for i in range(7):
            copy3(w, i).wait_send()
    second = split(dot3(split(chips[1].reshape(M, M)), split(chips[2].reshape(M, M))))
    after = dot3(split(chips[0].reshape(M, M)), second)
    later[...] = after

    @pl.when(core == 0)
    def _():
        later[...] = dot3(odd, split(after))

    tail = split(later[...])
    out_ref[1] = dot3(g1, tail).astype(BF16)
    out_ref[0] = dot3(split(own), tail).astype(BF16)
    for by in (1, 2, 3):
        @pl.when(x >= by)
        def _():
            copy_x(by).wait_send()
    for j in range(3):
        @pl.when(x <= j)
        def _():
            pass_on(j).wait_send()


def smooth_kernel(ens_ref, suffix_ref, out_ref, held, sem):
    steps = held.shape[0]
    rows = held.shape[1]
    each = steps // 2

    def copy(i):
        return pltpu.make_async_copy(held.at[i], out_ref.at[i // each, pl.ds((i % each) * rows, rows)], sem.at[i])

    for i in range(steps):
        block = ens_ref[i // each, (i % each) * rows : (i % each + 1) * rows, :]
        held[i] = dot(block, suffix_ref[i // each]).astype(BF16)
        copy(i).start()
    for i in range(steps):
        copy(i).wait()


def on_device(ensemble, obs_index, obs_value, obs_var):
    vmem = pl.BlockSpec(memory_space=pltpu.VMEM)
    sems = pltpu.SemaphoreType.DMA
    suffix = pl.pallas_call(
        suffix_kernel,
        out_shape=jax.ShapeDtypeStruct((2, M, M), BF16),
        in_specs=[vmem] * 4,
        out_specs=vmem,
        scratch_shapes=[
            pltpu.VMEM((2, 8, SENT, 128), F32),
            pltpu.VMEM((2, 7, SENT, 128), F32),
            pltpu.VMEM((2, SENT, 128), F32),
            pltpu.VMEM((2, 7, SENT, 128), F32),
            pltpu.VMEM((2, 8, SHARD, 128), F32),
            pltpu.VMEM((2, 8, 128), F32),
            pltpu.VMEM((2, M, M), F32),
            pltpu.VMEM((128, M), F32),
            pltpu.VMEM((3, 2, 128, M), F32),
            pltpu.VMEM((M, M), F32),
            sems((2, 7)), sems((2, 7)), sems((2, 7)), sems((2, 7)), sems((2, 7)), sems((2, 7)),
            sems, sems, sems((3,)), sems((3,)), sems((3,)), sems((3,)),
        ],
        compiler_params=pltpu.CompilerParams(collective_id=0, has_side_effects=True, vmem_limit_bytes=VMEM_LIMIT),
        name="suffixes",
    )(ensemble, obs_index, obs_value, obs_var)
    return pl.pallas_call(
        smooth_kernel,
        out_shape=jax.ShapeDtypeStruct(ensemble.shape, BF16),
        in_specs=[vmem] * 2,
        out_specs=pl.BlockSpec(memory_space=pltpu.HBM),
        scratch_shapes=[pltpu.VMEM((8, ensemble.shape[1] // 4, M), BF16), sems((8,))],
        compiler_params=pltpu.CompilerParams(vmem_limit_bytes=VMEM_LIMIT),
        name="smooth",
    )(ensemble, suffix)


def solution(mesh):
    placed = (P("tm", "space", None), P("tm", "space"), P("tm", "space"), P("tm", "space"))
    return jax.shard_map(
        on_device, mesh=mesh, in_specs=placed, out_specs=P("tm", "space", None), check_vma=False
    )
```

```python
import jax
import jax.numpy as jnp
from jax import lax
from jax.experimental import pallas as pl
from jax.experimental.pallas import tpu as pltpu
from jax.sharding import PartitionSpec as P

NS_ITERS = 6
M = 256
MESH = pl.DeviceIdType.MESH
F32 = jnp.float32
BF16 = jnp.bfloat16
ORDER = (4, 3, 5, 2, 6, 1, 7)
SHARD = 32
SENT = 40
VMEM_LIMIT = 20 * 2**20


def dot(a, b):
    return jnp.dot(a, b, preferred_element_type=F32)


def dot_nt(a, b):
    return lax.dot_general(a, b, (((1,), (1,)), ((), ())), preferred_element_type=F32)


def dot_tn(a, b):
    return lax.dot_general(a, b, (((0,), (0,)), ((), ())), preferred_element_type=F32)


def split(a):
    high = a.astype(BF16)
    return high, (a - high.astype(F32)).astype(BF16)


def dot3(a, b):
    left = jnp.concatenate([a[0], a[1], a[0]], axis=1)
    right = jnp.concatenate([b[0], b[0], b[1]], axis=0)
    return dot(left, right)


def local_sums(ens, index, value, var):
    inv = 1.0 / var
    low = index & 127
    high = index >> 7
    count = index.shape[1]
    at_low = jnp.where(lax.broadcasted_iota(jnp.int32, (128, count), 0) == low, 1.0, 0.0).astype(BF16)
    at_high = lax.broadcasted_iota(jnp.int32, (16, count), 0) == high
    terms = jnp.concatenate([jnp.where(at_high, inv, 0.0), jnp.where(at_high, value * inv, 0.0)], axis=0)
    first = terms.astype(BF16)
    rest = terms - first.astype(F32)
    second = rest.astype(BF16)
    third = (rest - second.astype(F32)).astype(BF16)
    columns = dot_nt(at_low, first) + (dot_nt(at_low, second) + dot_nt(at_low, third))
    rows = dot_nt(first, at_low) + (dot_nt(second, at_low) + dot_nt(third, at_low))
    s_row = jnp.concatenate([rows[16 + i : 17 + i, :] for i in range(16)], axis=1)
    s_first, s_second = split(s_row)
    s_both = jnp.concatenate([s_first, s_second, jnp.zeros((14, s_row.shape[1]), BF16)], axis=0)
    scaled = [split(ens[128 * i : 128 * (i + 1), :].astype(F32) * columns[:, i : i + 1]) for i in range(16)]
    scaled_first = jnp.concatenate([a for a, _ in scaled], axis=0)
    scaled_second = jnp.concatenate([b for _, b in scaled], axis=0)
    gram = dot_tn(ens, scaled_first) + dot_tn(ens, scaled_second)
    proj = dot(s_both, ens)
    return gram, proj[0:1, :] + proj[1:2, :]


def pack(gram, proj):
    r = lax.broadcasted_iota(jnp.int32, (128, 128), 0)
    c = lax.broadcasted_iota(jnp.int32, (128, 128), 1)
    k11, k12, k22 = gram[:128, :128], gram[:128, 128:], gram[128:, 128:]
    mixed = jnp.where(r >= c, k11, k22)
    diag = jnp.sum(jnp.where(r == c, k22, 0.0), axis=0, keepdims=True)
    extra = jnp.concatenate([diag, proj[:, :128], proj[:, 128:], jnp.zeros((5, 128), F32)], axis=0)
    return jnp.concatenate([k12, mixed], axis=0), extra


def unpack(body, extra):
    r = lax.broadcasted_iota(jnp.int32, (128, 128), 0)
    c = lax.broadcasted_iota(jnp.int32, (128, 128), 1)
    k12, mixed = body[:128, :], body[128:, :]
    turned = mixed.T
    k11 = jnp.where(r >= c, mixed, turned)
    k22 = jnp.where(r < c, mixed, jnp.where(r == c, extra[0:1, :], turned))
    gram = jnp.concatenate(
        [jnp.concatenate([k11, k12], axis=1), jnp.concatenate([k12.T, k22], axis=1)], axis=0
    )
    return gram, jnp.concatenate([extra[1:2, :], extra[2:3, :]], axis=1)


def transforms(sums):
    r = lax.broadcasted_iota(jnp.int32, (M, M), 0)
    c = lax.broadcasted_iota(jnp.int32, (M, M), 1)
    eye = jnp.where(r == c, 1.0, 0.0).astype(F32)
    count = range(len(sums))
    scales, projs, y, z = [], [], [], []
    for gram, proj in sums:
        col_mean = jnp.mean(gram, axis=0, keepdims=True)
        row_mean = jnp.mean(gram, axis=1, keepdims=True)
        amat = gram - row_mean - (col_mean - jnp.mean(col_mean, axis=1, keepdims=True)) + (M - 1.0) * eye
        scale = jnp.sqrt(jnp.sum(jnp.sum(amat * amat, axis=0, keepdims=True), axis=1, keepdims=True))
        start = amat / scale
        proj = proj - col_mean
        projs.append(proj - jnp.mean(proj, axis=1, keepdims=True))
        scales.append(scale)
        y.append(split(start))
        z.append(split(1.5 * eye - 0.5 * start))
    y = [split(dot3(y[w], z[w])) for w in count]
    for step in range(1, NS_ITERS):
        t = [split(1.5 * eye - 0.5 * dot3(z[w], y[w])) for w in count]
        last = [dot3(t[w], z[w]) for w in count]
        z = [split(last[w]) for w in count]
        if step < NS_ITERS - 1:
            y = [split(dot3(y[w], t[w])) for w in count]
    gmats = []
    for w in count:
        vec = dot3(split(jnp.broadcast_to(projs[w], (16, M))), z[w])
        vec = split(vec)
        mean = dot_nt(z[w][0], vec[0]) + (dot_nt(z[w][0], vec[1]) + dot_nt(z[w][1], vec[0]))
        wmean = mean[:, 0:1] / scales[w]
        wmean = wmean - jnp.mean(wmean, axis=0, keepdims=True)
        wtrans = last[w] * (jnp.sqrt(M - 1.0) / jnp.sqrt(scales[w]))
        gmats.append(wmean + (wtrans - jnp.mean(wtrans, axis=0, keepdims=True) + 1.0 / M))
    return gmats


def suffix_kernel(
    ens_in, index_in, value_in, var_in, out_ref, ens_ref,
    index_ref, value_ref, var_ref, load, parts, got1, mine, got2, whole, extras, pair, half, chips, later,
    send1, recv1, send2, recv2, send3, recv3, core_send, core_recv, x_send, x_recv, f_send, f_recv,
):
    t = lax.axis_index("tm")
    s = lax.axis_index("space")
    x, core = t // 2, t % 2
    at = (s // 8, s % 8)

    def along(axis, by):
        spot = list(at)
        spot[axis] = (at[axis] + by) % 8
        return {"tm": t, "space": spot[0] * 8 + spot[1]}

    def on_x(by):
        return {"tm": ((x + by + 4) % 4) * 2 + core, "space": s}

    sibling = {"tm": x * 2 + 1 - core, "space": s}

    pairs = ((index_in, index_ref), (value_in, value_ref), (var_in, var_ref))
    loads = [pltpu.make_async_copy(a, b, load.at[i]) for i, (a, b) in enumerate(pairs)]
    loads += [pltpu.make_async_copy(ens_in.at[w], ens_ref.at[w], load.at[3 + w]) for w in range(2)]
    for copy in loads:
        copy.start()

    barrier = pltpu.get_barrier_semaphore()
    for by in ORDER:
        for axis in range(2):
            pl.semaphore_signal(barrier, inc=1, device_id=along(axis, by), device_id_type=MESH)
    for by in (1, 2, 3):
        pl.semaphore_signal(barrier, inc=1, device_id=on_x(by), device_id_type=MESH)
    pl.semaphore_signal(barrier, inc=1, device_id=sibling, device_id_type=MESH)

    def copy1(w, i):
        by = ORDER[i]
        return pltpu.make_async_remote_copy(
            src_ref=parts.at[w, (at[w] + by) % 8], dst_ref=got1.at[w, i], send_sem=send1.at[w, i],
            recv_sem=recv1.at[w, i], device_id=along(w, by), device_id_type=MESH,
        )

    def copy2(w, i):
        return pltpu.make_async_remote_copy(
            src_ref=mine.at[w], dst_ref=got2.at[w, i], send_sem=send2.at[w, i],
            recv_sem=recv2.at[w, i], device_id=along(1 - w, ORDER[i]), device_id_type=MESH,
        )

    def copy3(w, i):
        return pltpu.make_async_remote_copy(
            src_ref=whole.at[w, at[w]], dst_ref=whole.at[w, at[w]], send_sem=send3.at[w, i],
            recv_sem=recv3.at[w, i], device_id=along(w, ORDER[i]), device_id_type=MESH,
        )

    for copy in loads[:3]:
        copy.wait()
    for w in range(2):
        loads[3 + w].wait()
        gram, proj = local_sums(ens_ref[w], index_ref[w : w + 1, :], value_ref[w : w + 1, :], var_ref[w : w + 1, :])
        body, extra = pack(gram, proj)
        for k in range(8):
            parts[w, k, 0:SHARD, :] = body[SHARD * k : SHARD * (k + 1), :]
            parts[w, k, SHARD:SENT, :] = extra
        if w == 0:
            pl.semaphore_wait(barrier, 18)
        for i in range(7):
            copy1(w, i).start()

    for w in range(2):
        total = parts[w, at[w]]
        for i in range(7):
            copy1(w, i).wait_recv()
            total = total + got1[w, i]
        mine[w] = total
        for i in range(7):
            copy2(w, i).start()

    for w in range(2):
        total = mine[w]
        for i in range(7):
            copy2(w, i).wait_recv()
            total = total + got2[w, i]
        whole[w, at[w]] = total[:SHARD]
        extras[w] = total[SHARD:]
        for i in range(7):
            copy3(w, i).start()

    for w in range(2):
        for i in range(7):
            copy1(w, i).wait_send()
            copy2(w, i).wait_send()
    for w in range(2):
        for i in range(7):
            copy3(w, i).wait_recv()

    g0, g1 = transforms([unpack(whole[w].reshape(256, 128), extras[w]) for w in range(2)])
    g0, g1 = split(g0), split(g1)
    own = dot3(g0, g1)
    pair[core] = own
    swap = pltpu.make_async_remote_copy(
        src_ref=pair.at[core], dst_ref=pair.at[core], send_sem=core_send, recv_sem=core_recv,
        device_id=sibling, device_id_type=MESH,
    )
    swap.start()
    r = lax.broadcasted_iota(jnp.int32, (128, M), 0)
    c = lax.broadcasted_iota(jnp.int32, (128, M), 1)
    for j in range(3):
        @pl.when(j < x)
        def _():
            for h in range(2):
                chips[j, h] = jnp.where(r + 128 * h == c, 1.0, 0.0).astype(F32)
    swap.wait()
    odd = split(pair[1])
    half[...] = dot3(split(pair[0, pl.ds(pl.multiple_of(core * 128, 128), 128), :]), odd)

    def copy_x(by):
        return pltpu.make_async_remote_copy(
            src_ref=half, dst_ref=chips.at[x - 1, core], send_sem=x_send.at[by - 1], recv_sem=x_recv.at[x - 1],
            device_id=on_x(-by), device_id_type=MESH,
        )

    def arrived(j):
        return pltpu.make_async_remote_copy(
            src_ref=half, dst_ref=chips.at[j, core], send_sem=x_send.at[0], recv_sem=x_recv.at[j],
            device_id=sibling, device_id_type=MESH,
        )

    def pass_on(j):
        return pltpu.make_async_remote_copy(
            src_ref=chips.at[j, core], dst_ref=chips.at[j, core], send_sem=f_send.at[j], recv_sem=f_recv.at[j],
            device_id=sibling, device_id_type=MESH,
        )

    def passed(j):
        return pltpu.make_async_remote_copy(
            src_ref=chips.at[j, core], dst_ref=chips.at[j, 1 - core], send_sem=f_send.at[j], recv_sem=f_recv.at[j],
            device_id=sibling, device_id_type=MESH,
        )

    for by in (1, 2, 3):
        @pl.when(x >= by)
        def _():
            copy_x(by).start()
    for j in range(3):
        @pl.when(x <= j)
        def _():
            arrived(j).wait_recv()
            pass_on(j).start()
    for j in range(3):
        @pl.when(x <= j)
        def _():
            passed(j).wait_recv()
    for w in range(2):
        for i in range(7):
            copy3(w, i).wait_send()
    second = split(dot3(split(chips[1].reshape(M, M)), split(chips[2].reshape(M, M))))
    after = dot3(split(chips[0].reshape(M, M)), second)
    later[...] = after

    @pl.when(core == 0)
    def _():
        later[...] = dot3(odd, split(after))

    tail = split(later[...])
    out_ref[1] = dot3(g1, tail).astype(BF16)
    out_ref[0] = dot3(split(own), tail).astype(BF16)
    for by in (1, 2, 3):
        @pl.when(x >= by)
        def _():
            copy_x(by).wait_send()
    for j in range(3):
        @pl.when(x <= j)
        def _():
            pass_on(j).wait_send()


def smooth_kernel(ens_ref, suffix_ref, out_ref, held, sem):
    steps = held.shape[0]
    rows = held.shape[1]
    each = steps // 2

    def copy(i):
        return pltpu.make_async_copy(held.at[i], out_ref.at[i // each, pl.ds((i % each) * rows, rows)], sem.at[i])

    for i in range(steps):
        block = ens_ref[i // each, (i % each) * rows : (i % each + 1) * rows, :]
        held[i] = dot(block, suffix_ref[i // each]).astype(BF16)
        copy(i).start()
    for i in range(steps):
        copy(i).wait()


def on_device(ensemble, obs_index, obs_value, obs_var):
    vmem = pl.BlockSpec(memory_space=pltpu.VMEM)
    sems = pltpu.SemaphoreType.DMA
    small = [pltpu.VMEM(a.shape, a.dtype) for a in (obs_index, obs_value, obs_var)]
    suffix, held = pl.pallas_call(
        suffix_kernel,
        out_shape=(jax.ShapeDtypeStruct((2, M, M), BF16), jax.ShapeDtypeStruct(ensemble.shape, BF16)),
        in_specs=[pl.BlockSpec(memory_space=pltpu.HBM)] * 4,
        out_specs=(vmem, vmem),
        scratch_shapes=small + [
            sems((5,)),
            pltpu.VMEM((2, 8, SENT, 128), F32),
            pltpu.VMEM((2, 7, SENT, 128), F32),
            pltpu.VMEM((2, SENT, 128), F32),
            pltpu.VMEM((2, 7, SENT, 128), F32),
            pltpu.VMEM((2, 8, SHARD, 128), F32),
            pltpu.VMEM((2, 8, 128), F32),
            pltpu.VMEM((2, M, M), F32),
            pltpu.VMEM((128, M), F32),
            pltpu.VMEM((3, 2, 128, M), F32),
            pltpu.VMEM((M, M), F32),
            sems((2, 7)), sems((2, 7)), sems((2, 7)), sems((2, 7)), sems((2, 7)), sems((2, 7)),
            sems, sems, sems((3,)), sems((3,)), sems((3,)), sems((3,)),
        ],
        compiler_params=pltpu.CompilerParams(collective_id=0, has_side_effects=True, vmem_limit_bytes=VMEM_LIMIT),
        name="suffixes",
    )(*(pltpu.with_memory_space_constraint(a, pltpu.HBM) for a in (ensemble, obs_index, obs_value, obs_var)))
    return pl.pallas_call(
        smooth_kernel,
        out_shape=jax.ShapeDtypeStruct(ensemble.shape, BF16),
        in_specs=[vmem] * 2,
        out_specs=pl.BlockSpec(memory_space=pltpu.HBM),
        scratch_shapes=[pltpu.VMEM((8, ensemble.shape[1] // 4, M), BF16), sems((8,))],
        compiler_params=pltpu.CompilerParams(vmem_limit_bytes=VMEM_LIMIT),
        name="smooth",
    )(held, suffix)


def solution(mesh):
    placed = (P("tm", "space", None), P("tm", "space"), P("tm", "space"), P("tm", "space"))
    return jax.shard_map(
        on_device, mesh=mesh, in_specs=placed, out_specs=P("tm", "space", None), check_vma=False
    )
```

```python
import jax
import jax.numpy as jnp
from jax import lax
from jax.experimental import pallas as pl
from jax.experimental.pallas import tpu as pltpu
from jax.sharding import PartitionSpec as P

NS_ITERS = 6
M = 256
MESH = pl.DeviceIdType.MESH
F32 = jnp.float32
BF16 = jnp.bfloat16
ORDER = (4, 3, 5, 2, 6, 1, 7)
SHARD = 16
CHUNK = 64
VMEM_LIMIT = 20 * 2**20


def dot(a, b):
    return jnp.dot(a, b, preferred_element_type=F32)


def dot_nt(a, b):
    return lax.dot_general(a, b, (((1,), (1,)), ((), ())), preferred_element_type=F32)


def dot_tn(a, b):
    return lax.dot_general(a, b, (((0,), (0,)), ((), ())), preferred_element_type=F32)


def split(a):
    high = a.astype(BF16)
    return high, (a - high.astype(F32)).astype(BF16)


def dot3(a, b):
    left = jnp.concatenate([a[0], a[1], a[0]], axis=1)
    right = jnp.concatenate([b[0], b[0], b[1]], axis=0)
    return dot(left, right)


def row_sums(index, value, var):
    inv = 1.0 / var
    low = index & 127
    high = index >> 7
    count = index.shape[1]
    at_low = jnp.where(lax.broadcasted_iota(jnp.int32, (128, count), 0) == low, 1.0, 0.0).astype(BF16)
    at_high = lax.broadcasted_iota(jnp.int32, (16, count), 0) == high
    terms = jnp.concatenate([jnp.where(at_high, inv, 0.0), jnp.where(at_high, value * inv, 0.0)], axis=0)
    first = terms.astype(BF16)
    rest = terms - first.astype(F32)
    second = rest.astype(BF16)
    third = (rest - second.astype(F32)).astype(BF16)
    columns = dot_nt(at_low, first) + (dot_nt(at_low, second) + dot_nt(at_low, third))
    rows = dot_nt(first, at_low) + (dot_nt(second, at_low) + dot_nt(third, at_low))
    s_row = jnp.concatenate([rows[16 + i : 17 + i, :] for i in range(16)], axis=1)
    s_first, s_second = split(s_row)
    return columns, jnp.concatenate([s_first, s_second, jnp.zeros((14, s_row.shape[1]), BF16)], axis=0)


def local_sums(ens, columns, s_both):
    scaled = [split(ens[128 * i : 128 * (i + 1), :].astype(F32) * columns[:, i : i + 1]) for i in range(16)]
    scaled_first = jnp.concatenate([a for a, _ in scaled], axis=0)
    scaled_second = jnp.concatenate([b for _, b in scaled], axis=0)
    gram = dot_tn(ens, scaled_first) + dot_tn(ens, scaled_second)
    proj = dot(s_both, ens)
    return gram, proj[0:1, :] + proj[1:2, :]


def pack(gram, proj):
    r = lax.broadcasted_iota(jnp.int32, (128, 128), 0)
    c = lax.broadcasted_iota(jnp.int32, (128, 128), 1)
    k11, k12, k22 = gram[:128, :128], gram[:128, 128:], gram[128:, 128:]
    mixed = jnp.where(r >= c, k11, k22)
    diag = jnp.sum(jnp.where(r == c, k22, 0.0), axis=0, keepdims=True)
    extra = jnp.concatenate([diag, proj[:, :128], proj[:, 128:], jnp.zeros((5, 128), F32)], axis=0)
    return k12, mixed, extra


def unpack(k12, mixed, extra):
    r = lax.broadcasted_iota(jnp.int32, (128, 128), 0)
    c = lax.broadcasted_iota(jnp.int32, (128, 128), 1)
    turned = mixed.T
    k11 = jnp.where(r >= c, mixed, turned)
    k22 = jnp.where(r < c, mixed, jnp.where(r == c, extra[0:1, :], turned))
    gram = jnp.concatenate(
        [jnp.concatenate([k11, k12], axis=1), jnp.concatenate([k12.T, k22], axis=1)], axis=0
    )
    return gram, jnp.concatenate([extra[1:2, :], extra[2:3, :]], axis=1)


def transforms(sums):
    r = lax.broadcasted_iota(jnp.int32, (M, M), 0)
    c = lax.broadcasted_iota(jnp.int32, (M, M), 1)
    eye = jnp.where(r == c, 1.0, 0.0).astype(F32)
    count = range(len(sums))

    def twice(a, b):
        return dot(jnp.concatenate([a, a], axis=1), jnp.concatenate(b, axis=0))

    def after(a, b):
        return dot(jnp.concatenate(a, axis=1), jnp.concatenate([b, b], axis=0))

    scales, projs, y, z = [], [], [], []
    for gram, proj in sums:
        col_mean = jnp.mean(gram, axis=0, keepdims=True)
        row_mean = jnp.mean(gram, axis=1, keepdims=True)
        amat = gram - row_mean - (col_mean - jnp.mean(col_mean, axis=1, keepdims=True)) + (M - 1.0) * eye
        scale = jnp.sqrt(jnp.sum(jnp.sum(amat * amat, axis=0, keepdims=True), axis=1, keepdims=True))
        start = amat * (1.0 / scale)
        proj = proj - col_mean
        projs.append(proj - jnp.mean(proj, axis=1, keepdims=True))
        scales.append(scale)
        b = (0.5 * start).astype(BF16)
        y.append(1.5 * start - after(split(start), b))
        z.append(1.5 * eye - b.astype(F32))
    for step in range(1, NS_ITERS - 1):
        zs, ys = [split(a) for a in z], [split(a) for a in y]
        b = [(0.5 * dot(zs[w][0], ys[w][0])).astype(BF16) for w in count]
        z = [1.5 * z[w] - twice(b[w], zs[w]) for w in count]
        y = [1.5 * y[w] - after(ys[w], b[w]) for w in count]
    zs, ys = [split(a) for a in z], [split(a) for a in y]
    t = [split(1.5 * eye - 0.5 * dot3(zs[w], ys[w])) for w in count]
    z = [dot3(t[w], zs[w]) for w in count]
    turned = []
    for w in count:
        both = split(z[w])
        vec = dot3(split(jnp.broadcast_to(projs[w], (16, M))), both)
        wmean = dot3(split(vec), both)[0:1, :] / scales[w]
        wmean = wmean - jnp.mean(wmean, axis=1, keepdims=True)
        wtrans = z[w] * (jnp.sqrt(M - 1.0) / jnp.sqrt(scales[w]))
        turned.append(wtrans - jnp.mean(wtrans, axis=1, keepdims=True) + (wmean + 1.0 / M))
    return turned


def suffix_kernel(
    ens_in, index_in, value_in, var_in, out_ref, ens_ref,
    index_ref, value_ref, var_ref, load, parts, got1, mine, got2, whole, extras, pair, half, chips, tail,
    send1, recv1, send2, recv2, send3, recv3, core_send, core_recv, x_send, x_recv, f_send, f_recv,
):
    t = lax.axis_index("tm")
    s = lax.axis_index("space")
    x, core = t // 2, t % 2
    at = (s // 8, s % 8)

    def along(axis, by):
        spot = list(at)
        spot[axis] = (at[axis] + by) % 8
        return {"tm": t, "space": spot[0] * 8 + spot[1]}

    def on_x(by):
        return {"tm": ((x + by + 4) % 4) * 2 + core, "space": s}

    sibling = {"tm": x * 2 + 1 - core, "space": s}

    pairs = ((index_in, index_ref), (value_in, value_ref), (var_in, var_ref))
    loads = [pltpu.make_async_copy(a, b, load.at[i]) for i, (a, b) in enumerate(pairs)]
    loads += [pltpu.make_async_copy(ens_in.at[w], ens_ref.at[w], load.at[3 + w]) for w in range(2)]
    for copy in loads:
        copy.start()

    barrier = pltpu.get_barrier_semaphore()
    for by in ORDER:
        for axis in range(2):
            pl.semaphore_signal(barrier, inc=1, device_id=along(axis, by), device_id_type=MESH)
    for by in (1, 2, 3):
        pl.semaphore_signal(barrier, inc=1, device_id=on_x(by), device_id_type=MESH)
    pl.semaphore_signal(barrier, inc=1, device_id=sibling, device_id_type=MESH)

    blocks = [(w, p) for w in range(2) for p in range(2)]

    def axis_of(w, p):
        return (w + p) % 2

    def sent(p):
        return pl.ds(0, SHARD + 8 * p)

    def copy1(w, p, i):
        axis, by = axis_of(w, p), ORDER[i]
        return pltpu.make_async_remote_copy(
            src_ref=parts.at[w, p, (at[axis] + by) % 8, sent(p)], dst_ref=got1.at[w, p, i, sent(p)],
            send_sem=send1.at[w, p, i], recv_sem=recv1.at[w, p, i], device_id=along(axis, by), device_id_type=MESH,
        )

    def copy2(w, p, i):
        return pltpu.make_async_remote_copy(
            src_ref=mine.at[w, p, sent(p)], dst_ref=got2.at[w, p, i, sent(p)],
            send_sem=send2.at[w, p, i], recv_sem=recv2.at[w, p, i],
            device_id=along(1 - axis_of(w, p), ORDER[i]), device_id_type=MESH,
        )

    def copy3(w, p, i):
        axis = axis_of(w, p)
        return pltpu.make_async_remote_copy(
            src_ref=whole.at[w, p, at[axis]], dst_ref=whole.at[w, p, at[axis]],
            send_sem=send3.at[w, p, i], recv_sem=recv3.at[w, p, i], device_id=along(axis, ORDER[i]), device_id_type=MESH,
        )

    for copy in loads[:3]:
        copy.wait()
    sums = [row_sums(index_ref[w : w + 1, :], value_ref[w : w + 1, :], var_ref[w : w + 1, :]) for w in range(2)]
    for w in range(2):
        loads[3 + w].wait()
        k12, mixed, extra = pack(*local_sums(ens_ref[w], *sums[w]))
        for k in range(8):
            parts[w, 0, k, 0:SHARD, :] = k12[SHARD * k : SHARD * (k + 1), :]
            parts[w, 1, k, 0:SHARD, :] = mixed[SHARD * k : SHARD * (k + 1), :]
            parts[w, 1, k, SHARD:, :] = extra
        if w == 0:
            pl.semaphore_wait(barrier, 18)
        for i in range(7):
            for p in range(2):
                copy1(w, p, i).start()

    for w, p in blocks:
        total = parts[w, p, at[axis_of(w, p)], sent(p)]
        for i in range(7):
            copy1(w, p, i).wait_recv()
            total = total + got1[w, p, i, sent(p)]
        mine[w, p, sent(p)] = total
        for i in range(7):
            copy2(w, p, i).start()

    for w, p in blocks:
        total = mine[w, p, sent(p)]
        for i in range(7):
            copy2(w, p, i).wait_recv()
            total = total + got2[w, p, i, sent(p)]
        whole[w, p, at[axis_of(w, p)]] = total[:SHARD]
        if p == 1:
            extras[w] = total[SHARD:]
        for i in range(7):
            copy3(w, p, i).start()

    for w, p in blocks:
        for i in range(7):
            copy1(w, p, i).wait_send()
    for w, p in blocks:
        for i in range(7):
            copy3(w, p, i).wait_recv()

    h0, h1 = transforms(
        [unpack(whole[w, 0].reshape(128, 128), whole[w, 1].reshape(128, 128), extras[w]) for w in range(2)]
    )
    h0, h1 = split(h0), split(h1)
    own = dot3(h1, h0)
    pair[core] = own
    swap = pltpu.make_async_remote_copy(
        src_ref=pair.at[core], dst_ref=pair.at[core], send_sem=core_send, recv_sem=core_recv,
        device_id=sibling, device_id_type=MESH,
    )
    swap.start()
    for w, p in blocks:
        for i in range(7):
            copy2(w, p, i).wait_send()
    for w, p in blocks:
        for i in range(7):
            copy3(w, p, i).wait_send()
    swap.wait()
    even = split(pair[0])

    def copy_x(by, n):
        rows = pl.ds(CHUNK * n, CHUNK)
        return pltpu.make_async_remote_copy(
            src_ref=half.at[rows], dst_ref=chips.at[x - 1, core, rows], send_sem=x_send.at[by - 1, n],
            recv_sem=x_recv.at[x - 1, n], device_id=on_x(-by), device_id_type=MESH,
        )

    def arrived(j, n):
        rows = pl.ds(CHUNK * n, CHUNK)
        return pltpu.make_async_remote_copy(
            src_ref=half.at[rows], dst_ref=chips.at[j, core, rows], send_sem=x_send.at[0, n],
            recv_sem=x_recv.at[j, n], device_id=sibling, device_id_type=MESH,
        )

    def pass_on(j, n):
        rows = pl.ds(CHUNK * n, CHUNK)
        return pltpu.make_async_remote_copy(
            src_ref=chips.at[j, core, rows], dst_ref=chips.at[j, core, rows], send_sem=f_send.at[j, n],
            recv_sem=f_recv.at[j, n], device_id=sibling, device_id_type=MESH,
        )

    def passed(j, n):
        rows = pl.ds(CHUNK * n, CHUNK)
        return pltpu.make_async_remote_copy(
            src_ref=chips.at[j, core, rows], dst_ref=chips.at[j, 1 - core, rows], send_sem=f_send.at[j, n],
            recv_sem=f_recv.at[j, n], device_id=sibling, device_id_type=MESH,
        )

    for n in range(128 // CHUNK):
        top = pl.multiple_of(core * 128 + CHUNK * n, CHUNK)
        half[CHUNK * n : CHUNK * (n + 1), :] = dot3(split(pair[1, pl.ds(top, CHUNK), :]), even)
        for by in (2, 3, 1):
            @pl.when(x >= by)
            def _():
                copy_x(by, n).start()

    @pl.when(core == 0)
    def _():
        odd = split(pair[1])
        tail[:, :M] = dot3(odd, even)
        tail[:, M:] = dot3(odd, h1)

    @pl.when(core == 1)
    def _():
        tail[:, :M] = pair[1]
        tail[:, M:] = h1[0].astype(F32) + h1[1].astype(F32)

    for n in range(128 // CHUNK):
        for j in range(3):
            @pl.when(x <= j)
            def _():
                arrived(j, n).wait_recv()
                pass_on(j, n).start()
    for j in range(3):
        @pl.when(x <= j)
        def _():
            for n in range(128 // CHUNK):
                passed(j, n).wait_recv()
            tail[...] = dot3(split(chips[j].reshape(M, M)), split(tail[...]))
    out_ref[0] = tail[:, :M].astype(BF16)
    out_ref[1] = tail[:, M:].astype(BF16)
    for n in range(128 // CHUNK):
        for by in (1, 2, 3):
            @pl.when(x >= by)
            def _():
                copy_x(by, n).wait_send()
        for j in range(3):
            @pl.when(x <= j)
            def _():
                pass_on(j, n).wait_send()


def smooth_kernel(ens_ref, suffix_ref, out_ref, held, sem):
    steps = held.shape[0]
    rows = held.shape[1]
    each = steps // 2

    def copy(i):
        return pltpu.make_async_copy(held.at[i], out_ref.at[i // each, pl.ds((i % each) * rows, rows)], sem.at[i])

    for i in range(steps):
        block = ens_ref[i // each, (i % each) * rows : (i % each + 1) * rows, :]
        held[i] = dot_nt(block, suffix_ref[i // each]).astype(BF16)
        copy(i).start()
    for i in range(steps):
        copy(i).wait()


def on_device(ensemble, obs_index, obs_value, obs_var):
    vmem = pl.BlockSpec(memory_space=pltpu.VMEM)
    sems = pltpu.SemaphoreType.DMA
    small = [pltpu.VMEM(a.shape, a.dtype) for a in (obs_index, obs_value, obs_var)]
    suffix, held = pl.pallas_call(
        suffix_kernel,
        out_shape=(jax.ShapeDtypeStruct((2, M, M), BF16), jax.ShapeDtypeStruct(ensemble.shape, BF16)),
        in_specs=[pl.BlockSpec(memory_space=pltpu.HBM)] * 4,
        out_specs=(vmem, vmem),
        scratch_shapes=small + [
            sems((5,)),
            pltpu.VMEM((2, 2, 8, SHARD + 8, 128), F32),
            pltpu.VMEM((2, 2, 7, SHARD + 8, 128), F32),
            pltpu.VMEM((2, 2, SHARD + 8, 128), F32),
            pltpu.VMEM((2, 2, 7, SHARD + 8, 128), F32),
            pltpu.VMEM((2, 2, 8, SHARD, 128), F32),
            pltpu.VMEM((2, 8, 128), F32),
            pltpu.VMEM((2, M, M), F32),
            pltpu.VMEM((128, M), F32),
            pltpu.VMEM((3, 2, 128, M), F32),
            pltpu.VMEM((M, 2 * M), F32),
            sems((2, 2, 7)), sems((2, 2, 7)), sems((2, 2, 7)), sems((2, 2, 7)), sems((2, 2, 7)), sems((2, 2, 7)),
            sems, sems, sems((3, 128 // CHUNK)), sems((3, 128 // CHUNK)), sems((3, 128 // CHUNK)), sems((3, 128 // CHUNK)),
        ],
        compiler_params=pltpu.CompilerParams(collective_id=0, has_side_effects=True, vmem_limit_bytes=VMEM_LIMIT),
        name="suffixes",
    )(*(pltpu.with_memory_space_constraint(a, pltpu.HBM) for a in (ensemble, obs_index, obs_value, obs_var)))
    return pl.pallas_call(
        smooth_kernel,
        out_shape=jax.ShapeDtypeStruct(ensemble.shape, BF16),
        in_specs=[vmem] * 2,
        out_specs=pl.BlockSpec(memory_space=pltpu.HBM),
        scratch_shapes=[pltpu.VMEM((8, ensemble.shape[1] // 4, M), BF16), sems((8,))],
        compiler_params=pltpu.CompilerParams(vmem_limit_bytes=VMEM_LIMIT),
        name="smooth",
    )(held, suffix)


def solution(mesh):
    placed = (P("tm", "space", None), P("tm", "space"), P("tm", "space"), P("tm", "space"))
    return jax.shard_map(
        on_device, mesh=mesh, in_specs=placed, out_specs=P("tm", "space", None), check_vma=False
    )
```

```python
import jax
import jax.numpy as jnp
from jax import lax
from jax.experimental import pallas as pl
from jax.experimental.pallas import tpu as pltpu
from jax.sharding import PartitionSpec as P

NS_ITERS = 6
M = 256
MESH = pl.DeviceIdType.MESH
F32 = jnp.float32
BF16 = jnp.bfloat16
ORDER = (4, 3, 5, 2, 6, 1, 7)
SHARD = 16
CHUNK = 32
CHUNKS = 128 // CHUNK
VMEM_LIMIT = 20 * 2**20


def dot(a, b):
    return jnp.dot(a, b, preferred_element_type=F32)


def dot_nt(a, b):
    return lax.dot_general(a, b, (((1,), (1,)), ((), ())), preferred_element_type=F32)


def split(a):
    high = a.astype(BF16)
    return high, (a - high.astype(F32)).astype(BF16)


def dot3(a, b):
    left = jnp.concatenate([a[0], a[1], a[0]], axis=1)
    right = jnp.concatenate([b[0], b[0], b[1]], axis=0)
    return dot(left, right)


def row_sums(index, value, var):
    inv = 1.0 / var
    low = index & 127
    high = index >> 7
    count = index.shape[1]
    at_low = jnp.where(lax.broadcasted_iota(jnp.int32, (128, count), 0) == low, 1.0, 0.0).astype(BF16)
    at_high = lax.broadcasted_iota(jnp.int32, (16, count), 0) == high
    terms = jnp.concatenate([jnp.where(at_high, inv, 0.0), jnp.where(at_high, value * inv, 0.0)], axis=0)
    first = terms.astype(BF16)
    rest = terms - first.astype(F32)
    second = rest.astype(BF16)
    third = (rest - second.astype(F32)).astype(BF16)
    rows = dot_nt(jnp.concatenate([first, second, third], axis=1), jnp.concatenate([at_low] * 3, axis=1))
    w_row = jnp.concatenate([rows[i : i + 1, :] for i in range(16)], axis=1)
    s_row = jnp.concatenate([rows[16 + i : 17 + i, :] for i in range(16)], axis=1)
    s_first, s_second = split(s_row)
    return w_row, jnp.concatenate([s_first, s_second, jnp.zeros((14, s_row.shape[1]), BF16)], axis=0)


def local_sums(ens, w_row, s_both):
    first, second = split(ens.T.astype(F32) * w_row)
    proj = dot(s_both, ens)
    return dot(first, ens) + dot(second, ens), proj[0:1, :] + proj[1:2, :]


def pack(gram, proj):
    r = lax.broadcasted_iota(jnp.int32, (128, 128), 0)
    c = lax.broadcasted_iota(jnp.int32, (128, 128), 1)
    k11, k12, k22 = gram[:128, :128], gram[:128, 128:], gram[128:, 128:]
    mixed = jnp.where(r >= c, k11, k22)
    diag = jnp.sum(jnp.where(r == c, k22, 0.0), axis=0, keepdims=True)
    extra = jnp.concatenate([diag, proj[:, :128], proj[:, 128:], jnp.zeros((5, 128), F32)], axis=0)
    return k12, mixed, extra


def unpack(k12, mixed, extra):
    r = lax.broadcasted_iota(jnp.int32, (128, 128), 0)
    c = lax.broadcasted_iota(jnp.int32, (128, 128), 1)
    turned = mixed.T
    k11 = jnp.where(r >= c, mixed, turned)
    k22 = jnp.where(r < c, mixed, jnp.where(r == c, extra[0:1, :], turned))
    gram = jnp.concatenate(
        [jnp.concatenate([k11, k12], axis=1), jnp.concatenate([k12.T, k22], axis=1)], axis=0
    )
    return gram, jnp.concatenate([extra[1:2, :], extra[2:3, :]], axis=1)


def transforms(sums):
    r = lax.broadcasted_iota(jnp.int32, (M, M), 0)
    c = lax.broadcasted_iota(jnp.int32, (M, M), 1)
    eye = jnp.where(r == c, 1.0, 0.0).astype(F32)
    count = range(len(sums))

    def twice(a, b):
        return dot(jnp.concatenate([a, a], axis=1), jnp.concatenate(b, axis=0))

    def after(a, b):
        return dot(jnp.concatenate(a, axis=1), jnp.concatenate([b, b], axis=0))

    scales, projs, y, z, before = [], [], [], [], []
    for gram, proj in sums:
        col_mean = jnp.mean(gram, axis=0, keepdims=True)
        row_mean = jnp.mean(gram, axis=1, keepdims=True)
        amat = gram - row_mean - (col_mean - jnp.mean(col_mean, axis=1, keepdims=True)) + (M - 1.0) * eye
        scale = jnp.sqrt(jnp.sum(jnp.sum(amat * amat, axis=0, keepdims=True), axis=1, keepdims=True))
        start = amat * (1.0 / scale)
        proj = proj - col_mean
        projs.append(proj - jnp.mean(proj, axis=1, keepdims=True))
        scales.append(scale)
        b = (0.5 * start).astype(BF16)
        y.append(1.5 * start - dot(start.astype(BF16), b))
        z.append(1.5 * eye - b.astype(F32))
        before.append(b)
    b = [(0.5 * dot(z[w].astype(BF16), y[w].astype(BF16))).astype(BF16) for w in count]
    z = [1.5 * z[w] - (1.5 * b[w].astype(F32) - dot(b[w], before[w])) for w in count]
    y = [1.5 * y[w] - dot(y[w].astype(BF16), b[w]) for w in count]
    for step in range(2, NS_ITERS - 1):
        zs, ys = [split(a) for a in z], [split(a) for a in y]
        b = [(0.5 * dot(zs[w][0], ys[w][0])).astype(BF16) for w in count]
        z = [1.5 * z[w] - twice(b[w], zs[w]) for w in count]
        y = [1.5 * y[w] - after(ys[w], b[w]) for w in count]
    zs, ys = [split(a) for a in z], [split(a) for a in y]
    t = [split(1.5 * eye - 0.5 * dot3(zs[w], ys[w])) for w in count]
    z = [dot3(t[w], zs[w]) for w in count]
    turned = []
    for w in count:
        both = split(z[w])
        vec = dot3(split(jnp.broadcast_to(projs[w], (16, M))), both)
        wmean = dot3(split(vec), both)[0:1, :] / scales[w]
        wmean = wmean - jnp.mean(wmean, axis=1, keepdims=True)
        wtrans = z[w] * (jnp.sqrt(M - 1.0) / jnp.sqrt(scales[w]))
        turned.append(wtrans - jnp.mean(wtrans, axis=1, keepdims=True) + (wmean + 1.0 / M))
    return turned


def suffix_kernel(
    ens_in, index_in, value_in, var_in, out_ref, ens_ref,
    index_ref, value_ref, var_ref, load, parts, got1, mine, got2, whole, extras, pair, half, chips, tail,
    send1, recv1, send2, recv2, send3, recv3, core_send, core_recv, x_send, x_recv, f_send, f_recv, last, relay_send,
):
    t = lax.axis_index("tm")
    s = lax.axis_index("space")
    x, core = t // 2, t % 2
    at = (s // 8, s % 8)

    def along(axis, by):
        spot = list(at)
        spot[axis] = (at[axis] + by) % 8
        return {"tm": t, "space": spot[0] * 8 + spot[1]}

    def on_x(by):
        return {"tm": ((x + by + 4) % 4) * 2 + core, "space": s}

    sibling = {"tm": x * 2 + 1 - core, "space": s}

    pairs = ((index_in, index_ref), (value_in, value_ref), (var_in, var_ref))
    loads = [pltpu.make_async_copy(a, b, load.at[i]) for i, (a, b) in enumerate(pairs)]
    loads += [pltpu.make_async_copy(ens_in.at[w], ens_ref.at[w], load.at[3 + w]) for w in range(2)]
    for copy in loads:
        copy.start()

    barrier = pltpu.get_barrier_semaphore()
    for by in ORDER:
        for axis in range(2):
            pl.semaphore_signal(barrier, inc=1, device_id=along(axis, by), device_id_type=MESH)
    for by in (1, 2, 3):
        pl.semaphore_signal(barrier, inc=1, device_id=on_x(by), device_id_type=MESH)
    pl.semaphore_signal(barrier, inc=1, device_id=sibling, device_id_type=MESH)

    blocks = [(w, p) for w in range(2) for p in range(2)]

    def axis_of(w, p):
        return (w + p) % 2

    def sent(p):
        return pl.ds(0, SHARD + 8 * p)

    def copy1(w, p, i):
        axis, by = axis_of(w, p), ORDER[i]
        return pltpu.make_async_remote_copy(
            src_ref=parts.at[w, p, (at[axis] + by) % 8, sent(p)], dst_ref=got1.at[w, p, i, sent(p)],
            send_sem=send1.at[w, p, i], recv_sem=recv1.at[w, p, i], device_id=along(axis, by), device_id_type=MESH,
        )

    def copy2(w, p, i):
        return pltpu.make_async_remote_copy(
            src_ref=mine.at[w, p, sent(p)], dst_ref=got2.at[w, p, i, sent(p)],
            send_sem=send2.at[w, p, i], recv_sem=recv2.at[w, p, i],
            device_id=along(1 - axis_of(w, p), ORDER[i]), device_id_type=MESH,
        )

    def copy3(w, p, i):
        axis = axis_of(w, p)
        return pltpu.make_async_remote_copy(
            src_ref=whole.at[w, p, at[axis]], dst_ref=whole.at[w, p, at[axis]],
            send_sem=send3.at[w, p, i], recv_sem=recv3.at[w, p, i], device_id=along(axis, ORDER[i]), device_id_type=MESH,
        )

    for copy in loads[:3]:
        copy.wait()
    sums = [row_sums(index_ref[w : w + 1, :], value_ref[w : w + 1, :], var_ref[w : w + 1, :]) for w in range(2)]
    for w in range(2):
        loads[3 + w].wait()
        k12, mixed, extra = pack(*local_sums(ens_ref[w], *sums[w]))
        for k in range(8):
            parts[w, 0, k, 0:SHARD, :] = k12[SHARD * k : SHARD * (k + 1), :]
            parts[w, 1, k, 0:SHARD, :] = mixed[SHARD * k : SHARD * (k + 1), :]
            parts[w, 1, k, SHARD:, :] = extra
        if w == 0:
            pl.semaphore_wait(barrier, 18)
        for i in range(7):
            for p in range(2):
                copy1(w, p, i).start()

    for w, p in blocks:
        total = parts[w, p, at[axis_of(w, p)], sent(p)]
        for i in range(7):
            copy1(w, p, i).wait_recv()
            total = total + got1[w, p, i, sent(p)]
        mine[w, p, sent(p)] = total
        for i in range(7):
            copy2(w, p, i).start()

    for w, p in blocks:
        total = mine[w, p, sent(p)]
        for i in range(7):
            copy2(w, p, i).wait_recv()
            total = total + got2[w, p, i, sent(p)]
        whole[w, p, at[axis_of(w, p)]] = total[:SHARD]
        if p == 1:
            extras[w] = total[SHARD:]
        for i in range(7):
            copy3(w, p, i).start()

    for w, p in blocks:
        for i in range(7):
            copy1(w, p, i).wait_send()
    for w, p in blocks:
        for i in range(7):
            copy3(w, p, i).wait_recv()

    h0, h1 = transforms(
        [unpack(whole[w, 0].reshape(128, 128), whole[w, 1].reshape(128, 128), extras[w]) for w in range(2)]
    )
    h0, h1 = split(h0), split(h1)
    own = dot3(h1, h0)
    pair[core] = own
    swap = pltpu.make_async_remote_copy(
        src_ref=pair.at[core], dst_ref=pair.at[core], send_sem=core_send, recv_sem=core_recv,
        device_id=sibling, device_id_type=MESH,
    )
    swap.start()
    for w, p in blocks:
        for i in range(7):
            copy2(w, p, i).wait_send()
    for w, p in blocks:
        for i in range(7):
            copy3(w, p, i).wait_send()
    swap.wait()
    even = split(pair[0])

    def copy_x(by, n):
        rows = pl.ds(CHUNK * n, CHUNK)
        return pltpu.make_async_remote_copy(
            src_ref=half.at[rows], dst_ref=chips.at[x - 1, core, rows], send_sem=x_send.at[by - 1, n],
            recv_sem=x_recv.at[x - 1, n], device_id=on_x(-by), device_id_type=MESH,
        )

    def arrived(j, n):
        rows = pl.ds(CHUNK * n, CHUNK)
        return pltpu.make_async_remote_copy(
            src_ref=half.at[rows], dst_ref=chips.at[j, core, rows], send_sem=x_send.at[0, n],
            recv_sem=x_recv.at[j, n], device_id=sibling, device_id_type=MESH,
        )

    def pass_on(j, n):
        rows = pl.ds(CHUNK * n, CHUNK)
        return pltpu.make_async_remote_copy(
            src_ref=chips.at[j, core, rows], dst_ref=chips.at[j, core, rows], send_sem=f_send.at[j, n],
            recv_sem=f_recv.at[j, n], device_id=sibling, device_id_type=MESH,
        )

    def passed(j, n):
        rows = pl.ds(CHUNK * n, CHUNK)
        return pltpu.make_async_remote_copy(
            src_ref=chips.at[j, core, rows], dst_ref=chips.at[j, 1 - core, rows], send_sem=f_send.at[j, n],
            recv_sem=f_recv.at[j, n], device_id=sibling, device_id_type=MESH,
        )

    relay = pltpu.make_async_remote_copy(
        src_ref=chips.at[2 - x, core, pl.ds(0, CHUNK)], dst_ref=chips.at[2 - x, core, pl.ds(0, CHUNK)],
        send_sem=relay_send, recv_sem=x_recv.at[2 - x, 0], device_id={"tm": (1 - x) * 2 + core, "space": s},
        device_id_type=MESH,
    )

    for n in range(CHUNKS):
        top = pl.multiple_of(core * 128 + CHUNK * n, CHUNK)
        half[CHUNK * n : CHUNK * (n + 1), :] = dot3(split(pair[1, pl.ds(top, CHUNK), :]), even)
        for by in (2, 3, 1) if n else (3, 1):
            @pl.when(x >= by)
            def _():
                copy_x(by, n).start()

    @pl.when(core == 0)
    def _():
        odd = split(pair[1])
        tail[:, :M] = dot3(odd, even)
        tail[:, M:] = dot3(odd, h1)

    @pl.when(core == 1)
    def _():
        tail[:, :M] = pair[1]
        tail[:, M:] = h1[0].astype(F32) + h1[1].astype(F32)

    def receive(by, n):
        @pl.when(x + by <= 3)
        def _():
            arrived(x + by - 1, n).wait_recv()
            pass_on(x + by - 1, n).start()

    receive(1, 0)
    receive(3, 0)

    @pl.when(x <= 1)
    def _():
        relay.start()

    for n in range(1, CHUNKS):
        for by in (1, 3, 2):
            receive(by, n)
    receive(2, 0)

    def chip(j):
        for n in range(CHUNKS):
            passed(j, n).wait_recv()
        return split(chips[j].reshape(M, M))

    @pl.when(x == 0)
    def _():
        tail[...] = dot3(chip(0), split(tail[...]))

    @pl.when(x <= 1)
    def _():
        first = chip(1)

        @pl.when(x == 0)
        def _():
            last[...] = dot3(chip(2), first)

        @pl.when(x == 1)
        def _():
            tail[...] = dot3(first, split(tail[...]))

    @pl.when((x == 1) | (x == 2))
    def _():
        for n in range(CHUNKS):
            passed(2, n).wait_recv()
        last[...] = chips[2].reshape(M, M)

    @pl.when(x <= 2)
    def _():
        tail[...] = dot3(split(last[...]), split(tail[...]))

    out_ref[0] = tail[:, :M].astype(BF16)
    out_ref[1] = tail[:, M:].astype(BF16)

    @pl.when(x <= 1)
    def _():
        relay.wait_send()

    for n in range(CHUNKS):
        for by in (1, 2, 3) if n else (1, 3):
            @pl.when(x >= by)
            def _():
                copy_x(by, n).wait_send()
        for j in range(3):
            @pl.when(x <= j)
            def _():
                pass_on(j, n).wait_send()


def smooth_kernel(ens_ref, suffix_ref, out_ref, held, sem):
    steps = held.shape[0]
    rows = held.shape[1]
    each = steps // 2

    def copy(i):
        return pltpu.make_async_copy(held.at[i], out_ref.at[i // each, pl.ds((i % each) * rows, rows)], sem.at[i])

    for i in range(steps):
        block = ens_ref[i // each, (i % each) * rows : (i % each + 1) * rows, :]
        held[i] = dot_nt(block, suffix_ref[i // each]).astype(BF16)
        copy(i).start()
    for i in range(steps):
        copy(i).wait()


def on_device(ensemble, obs_index, obs_value, obs_var):
    vmem = pl.BlockSpec(memory_space=pltpu.VMEM)
    sems = pltpu.SemaphoreType.DMA
    small = [pltpu.VMEM(a.shape, a.dtype) for a in (obs_index, obs_value, obs_var)]
    suffix, held = pl.pallas_call(
        suffix_kernel,
        out_shape=(jax.ShapeDtypeStruct((2, M, M), BF16), jax.ShapeDtypeStruct(ensemble.shape, BF16)),
        in_specs=[pl.BlockSpec(memory_space=pltpu.HBM)] * 4,
        out_specs=(vmem, vmem),
        scratch_shapes=small + [
            sems((5,)),
            pltpu.VMEM((2, 2, 8, SHARD + 8, 128), F32),
            pltpu.VMEM((2, 2, 7, SHARD + 8, 128), F32),
            pltpu.VMEM((2, 2, SHARD + 8, 128), F32),
            pltpu.VMEM((2, 2, 7, SHARD + 8, 128), F32),
            pltpu.VMEM((2, 2, 8, SHARD, 128), F32),
            pltpu.VMEM((2, 8, 128), F32),
            pltpu.VMEM((2, M, M), F32),
            pltpu.VMEM((128, M), F32),
            pltpu.VMEM((3, 2, 128, M), F32),
            pltpu.VMEM((M, 2 * M), F32),
            sems((2, 2, 7)), sems((2, 2, 7)), sems((2, 2, 7)), sems((2, 2, 7)), sems((2, 2, 7)), sems((2, 2, 7)),
            sems, sems, sems((3, CHUNKS)), sems((3, CHUNKS)), sems((3, CHUNKS)), sems((3, CHUNKS)),
            pltpu.VMEM((M, M), F32), sems,
        ],
        compiler_params=pltpu.CompilerParams(collective_id=0, has_side_effects=True, vmem_limit_bytes=VMEM_LIMIT),
        name="suffixes",
    )(*(pltpu.with_memory_space_constraint(a, pltpu.HBM) for a in (ensemble, obs_index, obs_value, obs_var)))
    return pl.pallas_call(
        smooth_kernel,
        out_shape=jax.ShapeDtypeStruct(ensemble.shape, BF16),
        in_specs=[vmem] * 2,
        out_specs=pl.BlockSpec(memory_space=pltpu.HBM),
        scratch_shapes=[pltpu.VMEM((8, ensemble.shape[1] // 4, M), BF16), sems((8,))],
        compiler_params=pltpu.CompilerParams(vmem_limit_bytes=VMEM_LIMIT),
        name="smooth",
    )(held, suffix)


def solution(mesh):
    placed = (P("tm", "space", None), P("tm", "space"), P("tm", "space"), P("tm", "space"))
    return jax.shard_map(
        on_device, mesh=mesh, in_specs=placed, out_specs=P("tm", "space", None), check_vma=False
    )
```

```python
import jax
import jax.numpy as jnp
from jax import lax
from jax.experimental import pallas as pl
from jax.experimental.pallas import tpu as pltpu
from jax.sharding import PartitionSpec as P

NS_ITERS = 6
M = 256
MESH = pl.DeviceIdType.MESH
F32 = jnp.float32
BF16 = jnp.bfloat16
ORDER = (4, 3, 5, 2, 6, 1, 7)
SHARD = 16
CHUNK = 32
CHUNKS = 128 // CHUNK
RELAYED = 2
VMEM_LIMIT = 20 * 2**20


def dot(a, b):
    return jnp.dot(a, b, preferred_element_type=F32)


def dot_nt(a, b):
    return lax.dot_general(a, b, (((1,), (1,)), ((), ())), preferred_element_type=F32)


def split(a):
    high = a.astype(BF16)
    return high, (a - high.astype(F32)).astype(BF16)


def dot3(a, b):
    left = jnp.concatenate([a[0], a[1], a[0]], axis=1)
    right = jnp.concatenate([b[0], b[0], b[1]], axis=0)
    return dot(left, right)


def row_sums(index, value, var):
    inv = 1.0 / var
    low = index & 127
    high = index >> 7
    count = index.shape[1]
    at_low = jnp.where(lax.broadcasted_iota(jnp.int32, (128, count), 0) == low, 1.0, 0.0).astype(BF16)
    at_high = lax.broadcasted_iota(jnp.int32, (16, count), 0) == high
    terms = jnp.concatenate([jnp.where(at_high, inv, 0.0), jnp.where(at_high, value * inv, 0.0)], axis=0)
    first = terms.astype(BF16)
    rest = terms - first.astype(F32)
    second = rest.astype(BF16)
    third = (rest - second.astype(F32)).astype(BF16)
    rows = dot_nt(jnp.concatenate([first, second, third], axis=1), jnp.concatenate([at_low] * 3, axis=1))
    w_row = jnp.concatenate([rows[i : i + 1, :] for i in range(16)], axis=1)
    s_row = jnp.concatenate([rows[16 + i : 17 + i, :] for i in range(16)], axis=1)
    s_first, s_second = split(s_row)
    return w_row, jnp.concatenate([s_first, s_second, jnp.zeros((14, s_row.shape[1]), BF16)], axis=0)


def local_sums(ens, w_row, s_both):
    first, second = split(ens.T.astype(F32) * w_row)
    proj = dot(s_both, ens)
    return dot(first, ens) + dot(second, ens), proj[0:1, :] + proj[1:2, :]


def pack(gram, proj):
    r = lax.broadcasted_iota(jnp.int32, (128, 128), 0)
    c = lax.broadcasted_iota(jnp.int32, (128, 128), 1)
    k11, k12, k22 = gram[:128, :128], gram[:128, 128:], gram[128:, 128:]
    mixed = jnp.where(r >= c, k11, k22)
    diag = jnp.sum(jnp.where(r == c, k22, 0.0), axis=0, keepdims=True)
    extra = jnp.concatenate([diag, proj[:, :128], proj[:, 128:], jnp.zeros((5, 128), F32)], axis=0)
    return k12, mixed, extra


def unpack(k12, mixed, extra):
    r = lax.broadcasted_iota(jnp.int32, (128, 128), 0)
    c = lax.broadcasted_iota(jnp.int32, (128, 128), 1)
    turned = mixed.T
    k11 = jnp.where(r >= c, mixed, turned)
    k22 = jnp.where(r < c, mixed, jnp.where(r == c, extra[0:1, :], turned))
    gram = jnp.concatenate(
        [jnp.concatenate([k11, k12], axis=1), jnp.concatenate([k12.T, k22], axis=1)], axis=0
    )
    return gram, jnp.concatenate([extra[1:2, :], extra[2:3, :]], axis=1)


def transforms(sums):
    r = lax.broadcasted_iota(jnp.int32, (M, M), 0)
    c = lax.broadcasted_iota(jnp.int32, (M, M), 1)
    eye = jnp.where(r == c, 1.0, 0.0).astype(F32)
    count = range(len(sums))

    def twice(a, b):
        return dot(jnp.concatenate([a, a], axis=1), jnp.concatenate(b, axis=0))

    def after(a, b):
        return dot(jnp.concatenate(a, axis=1), jnp.concatenate([b, b], axis=0))

    scales, projs, y, z, before = [], [], [], [], []
    for gram, proj in sums:
        col_mean = jnp.mean(gram, axis=0, keepdims=True)
        row_mean = jnp.mean(gram, axis=1, keepdims=True)
        amat = gram - row_mean - (col_mean - jnp.mean(col_mean, axis=1, keepdims=True)) + (M - 1.0) * eye
        scale = jnp.sqrt(jnp.sum(jnp.sum(amat * amat, axis=0, keepdims=True), axis=1, keepdims=True))
        start = amat * (1.0 / scale)
        proj = proj - col_mean
        projs.append(proj - jnp.mean(proj, axis=1, keepdims=True))
        scales.append(scale)
        b = (0.5 * start).astype(BF16)
        y.append(1.5 * start - dot(start.astype(BF16), b))
        z.append(1.5 * eye - b.astype(F32))
        before.append(b)
    b = [(0.5 * dot(z[w].astype(BF16), y[w].astype(BF16))).astype(BF16) for w in count]
    z = [1.5 * z[w] - (1.5 * b[w].astype(F32) - dot(b[w], before[w])) for w in count]
    y = [1.5 * y[w] - dot(y[w].astype(BF16), b[w]) for w in count]
    for step in range(2, NS_ITERS - 1):
        zs, ys = [split(a) for a in z], [split(a) for a in y]
        b = [(0.5 * dot(zs[w][0], ys[w][0])).astype(BF16) for w in count]
        z = [1.5 * z[w] - twice(b[w], zs[w]) for w in count]
        y = [1.5 * y[w] - after(ys[w], b[w]) for w in count]
    zs, ys = [split(a) for a in z], [split(a) for a in y]
    t = [split(1.5 * eye - 0.5 * dot3(zs[w], ys[w])) for w in count]
    z = [dot3(t[w], zs[w]) for w in count]
    turned = []
    for w in count:
        both = split(z[w])
        vec = dot3(split(jnp.broadcast_to(projs[w], (16, M))), both)
        wmean = dot3(split(vec), both)[0:1, :] / scales[w]
        wmean = wmean - jnp.mean(wmean, axis=1, keepdims=True)
        wtrans = z[w] * (jnp.sqrt(M - 1.0) / jnp.sqrt(scales[w]))
        turned.append(wtrans - jnp.mean(wtrans, axis=1, keepdims=True) + (wmean + 1.0 / M))
    return turned


def suffix_kernel(
    ens_in, index_in, value_in, var_in, out_ref, ens_ref,
    index_ref, value_ref, var_ref, load, parts, got1, mine, got2, whole, extras, pair, half, chips, tail,
    send1, recv1, send2, recv2, send3, recv3, core_send, core_recv, x_send, x_recv, f_send, f_recv, last, relay_send,
    ext1, ext_mine, ext2, ext_all, ext_send, ext_recv1, ext_recv2, ext_recv3,
):
    t = lax.axis_index("tm")
    s = lax.axis_index("space")
    x, core = t // 2, t % 2
    at = (s // 8, s % 8)

    def along(axis, by):
        spot = list(at)
        spot[axis] = (at[axis] + by) % 8
        return {"tm": t, "space": spot[0] * 8 + spot[1]}

    def on_x(by):
        return {"tm": ((x + by + 4) % 4) * 2 + core, "space": s}

    sibling = {"tm": x * 2 + 1 - core, "space": s}

    pairs = ((index_in, index_ref), (value_in, value_ref), (var_in, var_ref))
    loads = [pltpu.make_async_copy(a, b, load.at[i]) for i, (a, b) in enumerate(pairs)]
    loads += [pltpu.make_async_copy(ens_in.at[w], ens_ref.at[w], load.at[3 + w]) for w in range(2)]
    for copy in loads:
        copy.start()

    barrier = pltpu.get_barrier_semaphore()
    for by in ORDER:
        for axis in range(2):
            pl.semaphore_signal(barrier, inc=1, device_id=along(axis, by), device_id_type=MESH)
    for by in (1, 2, 3):
        pl.semaphore_signal(barrier, inc=1, device_id=on_x(by), device_id_type=MESH)
    pl.semaphore_signal(barrier, inc=1, device_id=sibling, device_id_type=MESH)

    blocks = [(w, p) for w in range(2) for p in range(2)]

    def axis_of(w, p):
        return (w + p) % 2

    def copy1(w, p, i):
        axis, by = axis_of(w, p), ORDER[i]
        return pltpu.make_async_remote_copy(
            src_ref=parts.at[w, p, (at[axis] + by) % 8], dst_ref=got1.at[w, p, i],
            send_sem=send1.at[w, p, i], recv_sem=recv1.at[w, p, i], device_id=along(axis, by), device_id_type=MESH,
        )

    def copy2(w, p, i):
        return pltpu.make_async_remote_copy(
            src_ref=mine.at[w, p], dst_ref=got2.at[w, p, i],
            send_sem=send2.at[w, p, i], recv_sem=recv2.at[w, p, i],
            device_id=along(1 - axis_of(w, p), ORDER[i]), device_id_type=MESH,
        )

    def copy3(w, p, i):
        axis = axis_of(w, p)
        return pltpu.make_async_remote_copy(
            src_ref=whole.at[w, p, at[axis]], dst_ref=whole.at[w, p, at[axis]],
            send_sem=send3.at[w, p, i], recv_sem=recv3.at[w, p, i], device_id=along(axis, ORDER[i]), device_id_type=MESH,
        )

    def first_on(w):
        return at[axis_of(w, 1)] == 0

    def extra1(w):
        axis = axis_of(w, 1)
        return pltpu.make_async_remote_copy(
            src_ref=extras.at[w], dst_ref=ext1.at[w, at[axis] - 1], send_sem=ext_send.at[w, 0],
            recv_sem=ext_recv1.at[w, at[axis] - 1], device_id=along(axis, 8 - at[axis]), device_id_type=MESH,
        )

    def extra1_here(w, i):
        return pltpu.make_async_remote_copy(
            src_ref=extras.at[w], dst_ref=ext1.at[w, i], send_sem=ext_send.at[w, 0],
            recv_sem=ext_recv1.at[w, i], device_id=along(axis_of(w, 1), 1), device_id_type=MESH,
        )

    def extra2(w, i):
        return pltpu.make_async_remote_copy(
            src_ref=ext_mine.at[w], dst_ref=ext2.at[w, i], send_sem=ext_send.at[w, 1 + i],
            recv_sem=ext_recv2.at[w, i], device_id=along(1 - axis_of(w, 1), ORDER[i]), device_id_type=MESH,
        )

    def extra3(w, i):
        return pltpu.make_async_remote_copy(
            src_ref=ext_all.at[w], dst_ref=ext_all.at[w], send_sem=ext_send.at[w, 8 + i],
            recv_sem=ext_recv3.at[w], device_id=along(axis_of(w, 1), ORDER[i]), device_id_type=MESH,
        )

    for copy in loads[:3]:
        copy.wait()
    sums = [row_sums(index_ref[w : w + 1, :], value_ref[w : w + 1, :], var_ref[w : w + 1, :]) for w in range(2)]
    for w in range(2):
        loads[3 + w].wait()
        k12, mixed, extra = pack(*local_sums(ens_ref[w], *sums[w]))
        parts[w, 0] = k12.reshape(8, SHARD, 128)
        parts[w, 1] = mixed.reshape(8, SHARD, 128)
        extras[w] = extra
    pl.semaphore_wait(barrier, 18)
    for w in range(2):
        for i in range(7):
            for p in range(2):
                copy1(w, p, i).start()

        @pl.when(~first_on(w))
        def _():
            extra1(w).start()

    for w, p in blocks:
        total = parts[w, p, at[axis_of(w, p)]]
        for i in range(7):
            copy1(w, p, i).wait_recv()
            total = total + got1[w, p, i]
        mine[w, p] = total
        for i in range(7):
            copy2(w, p, i).start()
        if p == 1:
            @pl.when(first_on(w))
            def _():
                total = extras[w]
                for i in range(7):
                    extra1_here(w, i).wait_recv()
                    total = total + ext1[w, i]
                ext_mine[w] = total
                for i in range(7):
                    extra2(w, i).start()

    for w, p in blocks:
        total = mine[w, p]
        for i in range(7):
            copy2(w, p, i).wait_recv()
            total = total + got2[w, p, i]
        whole[w, p, at[axis_of(w, p)]] = total
        for i in range(7):
            copy3(w, p, i).start()
        if p == 1:
            @pl.when(first_on(w))
            def _():
                total = ext_mine[w]
                for i in range(7):
                    extra2(w, i).wait_recv()
                    total = total + ext2[w, i]
                ext_all[w] = total
                for i in range(7):
                    extra3(w, i).start()

    for w, p in blocks:
        for i in range(7):
            copy1(w, p, i).wait_send()
    for w, p in blocks:
        for i in range(7):
            copy3(w, p, i).wait_recv()
    for w in range(2):
        @pl.when(~first_on(w))
        def _():
            extra3(w, 0).wait_recv()

    h0, h1 = transforms(
        [unpack(whole[w, 0].reshape(128, 128), whole[w, 1].reshape(128, 128), ext_all[w]) for w in range(2)]
    )
    h0, h1 = split(h0), split(h1)
    own = dot3(h1, h0)
    pair[core] = own

    def swap(n):
        rows = pl.ds(128 * n, 128)
        return pltpu.make_async_remote_copy(
            src_ref=pair.at[core, rows], dst_ref=pair.at[core, rows], send_sem=core_send.at[n], recv_sem=core_recv.at[n],
            device_id=sibling, device_id_type=MESH,
        )

    swap(0).start()
    swap(1).start()
    for w, p in blocks:
        for i in range(7):
            copy2(w, p, i).wait_send()
            copy3(w, p, i).wait_send()
    for w in range(2):
        @pl.when(first_on(w))
        def _():
            for i in range(7):
                extra2(w, i).wait_send()
                extra3(w, i).wait_send()

        @pl.when(~first_on(w))
        def _():
            extra1(w).wait_send()

    swap(0).wait_recv()

    @pl.when(core == 1)
    def _():
        swap(1).wait_recv()

    even = split(pair[0])

    def copy_x(by, n):
        rows = pl.ds(CHUNK * n, CHUNK)
        return pltpu.make_async_remote_copy(
            src_ref=half.at[rows], dst_ref=chips.at[x - 1, core, rows], send_sem=x_send.at[by - 1, n],
            recv_sem=x_recv.at[x - 1, n], device_id=on_x(-by), device_id_type=MESH,
        )

    def arrived(j, n):
        rows = pl.ds(CHUNK * n, CHUNK)
        return pltpu.make_async_remote_copy(
            src_ref=half.at[rows], dst_ref=chips.at[j, core, rows], send_sem=x_send.at[0, n],
            recv_sem=x_recv.at[j, n], device_id=sibling, device_id_type=MESH,
        )

    def pass_on(j, n):
        rows = pl.ds(CHUNK * n, CHUNK)
        return pltpu.make_async_remote_copy(
            src_ref=chips.at[j, core, rows], dst_ref=chips.at[j, core, rows], send_sem=f_send.at[j, n],
            recv_sem=f_recv.at[j, n], device_id=sibling, device_id_type=MESH,
        )

    def passed(j, n):
        rows = pl.ds(CHUNK * n, CHUNK)
        return pltpu.make_async_remote_copy(
            src_ref=chips.at[j, core, rows], dst_ref=chips.at[j, 1 - core, rows], send_sem=f_send.at[j, n],
            recv_sem=f_recv.at[j, n], device_id=sibling, device_id_type=MESH,
        )

    def relay(n):
        rows = pl.ds(CHUNK * n, CHUNK)
        return pltpu.make_async_remote_copy(
            src_ref=chips.at[2 - x, core, rows], dst_ref=chips.at[2 - x, core, rows], send_sem=relay_send.at[n],
            recv_sem=x_recv.at[2 - x, n], device_id={"tm": (1 - x) * 2 + core, "space": s}, device_id_type=MESH,
        )

    for n in range(CHUNKS):
        top = pl.multiple_of(core * 128 + CHUNK * n, CHUNK)
        half[CHUNK * n : CHUNK * (n + 1), :] = dot3(split(pair[1, pl.ds(top, CHUNK), :]), even)
        for by in (2, 3, 1) if n >= RELAYED else (3, 1):
            @pl.when(x >= by)
            def _():
                copy_x(by, n).start()

    @pl.when(core == 0)
    def _():
        swap(1).wait_recv()
        odd = split(pair[1])
        tail[:, :M] = dot3(odd, even)
        tail[:, M:] = dot3(odd, h1)

    @pl.when(core == 1)
    def _():
        tail[:, :M] = pair[1]
        tail[:, M:] = h1[0].astype(F32) + h1[1].astype(F32)

    def receive(by, n):
        @pl.when(x + by <= 3)
        def _():
            arrived(x + by - 1, n).wait_recv()
            pass_on(x + by - 1, n).start()

    for n in range(CHUNKS):
        receive(1, n)
        receive(3, n)
        if n < RELAYED:
            @pl.when(x <= 1)
            def _():
                relay(n).start()
        else:
            receive(2, n)
    for n in range(RELAYED):
        receive(2, n)

    def chip(j):
        for n in range(CHUNKS):
            passed(j, n).wait_recv()
        return split(chips[j].reshape(M, M))

    @pl.when(x == 0)
    def _():
        tail[...] = dot3(chip(0), split(tail[...]))

    @pl.when(x <= 1)
    def _():
        first = chip(1)

        @pl.when(x == 0)
        def _():
            last[...] = dot3(chip(2), first)

        @pl.when(x == 1)
        def _():
            tail[...] = dot3(first, split(tail[...]))

    @pl.when((x == 1) | (x == 2))
    def _():
        for n in range(CHUNKS):
            passed(2, n).wait_recv()
        last[...] = chips[2].reshape(M, M)

    @pl.when(x <= 2)
    def _():
        tail[...] = dot3(split(last[...]), split(tail[...]))

    out_ref[0] = tail[:, :M].astype(BF16)
    out_ref[1] = tail[:, M:].astype(BF16)

    @pl.when(x <= 1)
    def _():
        for n in range(RELAYED):
            relay(n).wait_send()

    for n in range(2):
        swap(n).wait_send()
    for n in range(CHUNKS):
        for by in (1, 2, 3) if n >= RELAYED else (1, 3):
            @pl.when(x >= by)
            def _():
                copy_x(by, n).wait_send()
        for j in range(3):
            @pl.when(x <= j)
            def _():
                pass_on(j, n).wait_send()


def smooth_kernel(ens_ref, suffix_ref, out_ref, held, sem):
    steps = held.shape[0]
    rows = held.shape[1]
    each = steps // 2

    def copy(i):
        return pltpu.make_async_copy(held.at[i], out_ref.at[i // each, pl.ds((i % each) * rows, rows)], sem.at[i])

    for i in range(steps):
        block = ens_ref[i // each, (i % each) * rows : (i % each + 1) * rows, :]
        held[i] = dot_nt(block, suffix_ref[i // each]).astype(BF16)
        copy(i).start()
    for i in range(steps):
        copy(i).wait()


def on_device(ensemble, obs_index, obs_value, obs_var):
    vmem = pl.BlockSpec(memory_space=pltpu.VMEM)
    sems = pltpu.SemaphoreType.DMA
    small = [pltpu.VMEM(a.shape, a.dtype) for a in (obs_index, obs_value, obs_var)]
    suffix, held = pl.pallas_call(
        suffix_kernel,
        out_shape=(jax.ShapeDtypeStruct((2, M, M), BF16), jax.ShapeDtypeStruct(ensemble.shape, BF16)),
        in_specs=[pl.BlockSpec(memory_space=pltpu.HBM)] * 4,
        out_specs=(vmem, vmem),
        scratch_shapes=small + [
            sems((5,)),
            pltpu.VMEM((2, 2, 8, SHARD, 128), F32),
            pltpu.VMEM((2, 2, 7, SHARD, 128), F32),
            pltpu.VMEM((2, 2, SHARD, 128), F32),
            pltpu.VMEM((2, 2, 7, SHARD, 128), F32),
            pltpu.VMEM((2, 2, 8, SHARD, 128), F32),
            pltpu.VMEM((2, 8, 128), F32),
            pltpu.VMEM((2, M, M), F32),
            pltpu.VMEM((128, M), F32),
            pltpu.VMEM((3, 2, 128, M), F32),
            pltpu.VMEM((M, 2 * M), F32),
            sems((2, 2, 7)), sems((2, 2, 7)), sems((2, 2, 7)), sems((2, 2, 7)), sems((2, 2, 7)), sems((2, 2, 7)),
            sems((2,)), sems((2,)), sems((3, CHUNKS)), sems((3, CHUNKS)), sems((3, CHUNKS)), sems((3, CHUNKS)),
            pltpu.VMEM((M, M), F32), sems((RELAYED,)),
            pltpu.VMEM((2, 7, 8, 128), F32), pltpu.VMEM((2, 8, 128), F32),
            pltpu.VMEM((2, 7, 8, 128), F32), pltpu.VMEM((2, 8, 128), F32),
            sems((2, 15)), sems((2, 7)), sems((2, 7)), sems((2,)),
        ],
        compiler_params=pltpu.CompilerParams(collective_id=0, has_side_effects=True, vmem_limit_bytes=VMEM_LIMIT),
        name="suffixes",
    )(*(pltpu.with_memory_space_constraint(a, pltpu.HBM) for a in (ensemble, obs_index, obs_value, obs_var)))
    return pl.pallas_call(
        smooth_kernel,
        out_shape=jax.ShapeDtypeStruct(ensemble.shape, BF16),
        in_specs=[vmem] * 2,
        out_specs=pl.BlockSpec(memory_space=pltpu.HBM),
        scratch_shapes=[pltpu.VMEM((8, ensemble.shape[1] // 4, M), BF16), sems((8,))],
        compiler_params=pltpu.CompilerParams(vmem_limit_bytes=VMEM_LIMIT),
        name="smooth",
    )(held, suffix)


def solution(mesh):
    placed = (P("tm", "space", None), P("tm", "space"), P("tm", "space"), P("tm", "space"))
    return jax.shard_map(
        on_device, mesh=mesh, in_specs=placed, out_specs=P("tm", "space", None), check_vma=False
    )
```

```python
import jax
import jax.numpy as jnp
from jax import lax
from jax.experimental import pallas as pl
from jax.experimental.pallas import tpu as pltpu
from jax.sharding import PartitionSpec as P

NS_ITERS = 6
M = 256
MESH = pl.DeviceIdType.MESH
F32 = jnp.float32
BF16 = jnp.bfloat16
ORDER = (4, 3, 5, 2, 6, 1, 7)
SHARD = 16
CHUNK = 32
CHUNKS = 128 // CHUNK
RELAYED = 2
VMEM_LIMIT = 20 * 2**20


def dot(a, b):
    return jnp.dot(a, b, preferred_element_type=F32)


def dot_nt(a, b):
    return lax.dot_general(a, b, (((1,), (1,)), ((), ())), preferred_element_type=F32)


def split(a):
    high = a.astype(BF16)
    return high, (a - high.astype(F32)).astype(BF16)


def dot3(a, b):
    left = jnp.concatenate([a[0], a[1], a[0]], axis=1)
    right = jnp.concatenate([b[0], b[0], b[1]], axis=0)
    return dot(left, right)


def row_sums(index, value, var):
    inv = 1.0 / var
    low = index & 127
    high = index >> 7
    count = index.shape[1]
    at_low = jnp.where(lax.broadcasted_iota(jnp.int32, (128, count), 0) == low, 1.0, 0.0).astype(BF16)
    at_high = lax.broadcasted_iota(jnp.int32, (16, count), 0) == high
    terms = jnp.concatenate([jnp.where(at_high, inv, 0.0), jnp.where(at_high, value * inv, 0.0)], axis=0)
    first = terms.astype(BF16)
    rest = terms - first.astype(F32)
    second = rest.astype(BF16)
    third = (rest - second.astype(F32)).astype(BF16)
    rows = dot_nt(jnp.concatenate([first, second, third], axis=1), jnp.concatenate([at_low] * 3, axis=1))
    w_row = jnp.concatenate([rows[i : i + 1, :] for i in range(16)], axis=1)
    s_row = jnp.concatenate([rows[16 + i : 17 + i, :] for i in range(16)], axis=1)
    s_first, s_second = split(s_row)
    return w_row, jnp.concatenate([s_first, s_second, jnp.zeros((14, s_row.shape[1]), BF16)], axis=0)


def local_sums(ens, w_row, s_both):
    first, second = split(ens.T.astype(F32) * w_row)
    proj = dot(s_both, ens)
    return dot(first, ens) + dot(second, ens), proj[0:1, :] + proj[1:2, :]


def pack(gram, proj):
    r = lax.broadcasted_iota(jnp.int32, (128, 128), 0)
    c = lax.broadcasted_iota(jnp.int32, (128, 128), 1)
    k11, k12, k22 = gram[:128, :128], gram[:128, 128:], gram[128:, 128:]
    mixed = jnp.where(r >= c, k11, k22)
    diag = jnp.sum(jnp.where(r == c, k22, 0.0), axis=0, keepdims=True)
    extra = jnp.concatenate([diag, proj[:, :128], proj[:, 128:], jnp.zeros((5, 128), F32)], axis=0)
    return k12, mixed, extra


def unpack(k12, mixed, extra):
    r = lax.broadcasted_iota(jnp.int32, (128, 128), 0)
    c = lax.broadcasted_iota(jnp.int32, (128, 128), 1)
    turned = mixed.T
    k11 = jnp.where(r >= c, mixed, turned)
    k22 = jnp.where(r < c, mixed, jnp.where(r == c, extra[0:1, :], turned))
    gram = jnp.concatenate(
        [jnp.concatenate([k11, k12], axis=1), jnp.concatenate([k12.T, k22], axis=1)], axis=0
    )
    return gram, jnp.concatenate([extra[1:2, :], extra[2:3, :]], axis=1)


def identity():
    r = lax.broadcasted_iota(jnp.int32, (M, M), 0)
    c = lax.broadcasted_iota(jnp.int32, (M, M), 1)
    return jnp.where(r == c, 1.0, 0.0).astype(F32)


def begin(gram, proj):
    eye = identity()
    col_mean = jnp.mean(gram, axis=0, keepdims=True)
    row_mean = jnp.mean(gram, axis=1, keepdims=True)
    amat = gram - row_mean - (col_mean - jnp.mean(col_mean, axis=1, keepdims=True)) + (M - 1.0) * eye
    scale = jnp.sqrt(jnp.sum(jnp.sum(amat * amat, axis=0, keepdims=True), axis=1, keepdims=True))
    start = amat * (1.0 / scale)
    proj = proj - col_mean
    proj = proj - jnp.mean(proj, axis=1, keepdims=True)
    b = (0.5 * start).astype(BF16)
    return scale, proj, 1.5 * start - dot(start.astype(BF16), b), 1.5 * eye - b.astype(F32), b


def transforms(begun):
    eye = identity()
    count = range(len(begun))
    scales, projs, y, z, before = (list(a) for a in zip(*begun))

    def twice(a, b):
        return dot(jnp.concatenate([a, a], axis=1), jnp.concatenate(b, axis=0))

    def after(a, b):
        return dot(jnp.concatenate(a, axis=1), jnp.concatenate([b, b], axis=0))

    b = [(0.5 * dot(z[w].astype(BF16), y[w].astype(BF16))).astype(BF16) for w in count]
    z = [1.5 * z[w] - (1.5 * b[w].astype(F32) - dot(b[w], before[w])) for w in count]
    y = [1.5 * y[w] - dot(y[w].astype(BF16), b[w]) for w in count]
    for step in range(2, NS_ITERS - 1):
        zs, ys = [split(a) for a in z], [split(a) for a in y]
        b = [(0.5 * dot(zs[w][0], ys[w][0])).astype(BF16) for w in count]
        z = [1.5 * z[w] - twice(b[w], zs[w]) for w in count]
        y = [1.5 * y[w] - after(ys[w], b[w]) for w in count]
    zs, ys = [split(a) for a in z], [split(a) for a in y]
    t = [split(1.5 * eye - 0.5 * dot3(zs[w], ys[w])) for w in count]
    z = [dot3(t[w], zs[w]) for w in count]
    turned = []
    for w in count:
        both = split(z[w])
        vec = dot3(split(jnp.broadcast_to(projs[w], (16, M))), both)
        wmean = dot3(split(vec), both)[0:1, :] / scales[w]
        wmean = wmean - jnp.mean(wmean, axis=1, keepdims=True)
        wtrans = z[w] * (jnp.sqrt(M - 1.0) / jnp.sqrt(scales[w]))
        turned.append(wtrans - jnp.mean(wtrans, axis=1, keepdims=True) + (wmean + 1.0 / M))
    return turned


def suffix_kernel(
    ens_in, index_in, value_in, var_in, out_ref, ens_ref,
    index_ref, value_ref, var_ref, load, parts, got1, mine, got2, whole, extras, pair, half, chips, tail,
    send_1, recv1, send2, recv2, send3, recv3, core_send, core_recv, x_send, x_recv, f_send, f_recv, last, relay_send,
    ext1, ext_mine, ext2, ext_all, ext_send, ext_recv1, ext_recv2, ext_recv3, ready,
):
    t = lax.axis_index("tm")
    s = lax.axis_index("space")
    x, core = t // 2, t % 2
    at = (s // 8, s % 8)

    def along(axis, by):
        spot = list(at)
        spot[axis] = (at[axis] + by) % 8
        return {"tm": t, "space": spot[0] * 8 + spot[1]}

    def on_x(by):
        return {"tm": ((x + by + 4) % 4) * 2 + core, "space": s}

    sibling = {"tm": x * 2 + 1 - core, "space": s}

    pairs = ((index_in, index_ref), (value_in, value_ref), (var_in, var_ref))
    loads = [pltpu.make_async_copy(a, b, load.at[i]) for i, (a, b) in enumerate(pairs)]
    loads += [pltpu.make_async_copy(ens_in.at[w], ens_ref.at[w], load.at[3 + w]) for w in range(2)]
    for copy in loads:
        copy.start()

    barrier = pltpu.get_barrier_semaphore()
    for by in ORDER:
        for axis in range(2):
            there = {"tm": x * 2 + axis, "space": along(axis, by)["space"]}
            pl.semaphore_signal(barrier, inc=1, device_id=there, device_id_type=MESH)
    for by in (1, 2, 3):
        there = {"tm": ((x + by) % 4) * 2, "space": s}
        pl.semaphore_signal(barrier, inc=1, device_id=there, device_id_type=MESH)
    pl.semaphore_signal(barrier, inc=1, device_id=sibling, device_id_type=MESH)

    blocks = [(w, p) for w in range(2) for p in range(2)]

    def axis_of(w, p):
        return (w + p) % 2

    def copy1(w, p, i):
        axis, by = axis_of(w, p), ORDER[i]
        return pltpu.make_async_remote_copy(
            src_ref=parts.at[w, p, (at[axis] + by) % 8], dst_ref=got1.at[w, p, i],
            send_sem=send_1.at[w, p, i], recv_sem=recv1.at[w, p, i], device_id=along(axis, by), device_id_type=MESH,
        )

    def copy2(w, p, i):
        return pltpu.make_async_remote_copy(
            src_ref=mine.at[w, p], dst_ref=got2.at[w, p, i],
            send_sem=send2.at[w, p, i], recv_sem=recv2.at[w, p, i],
            device_id=along(1 - axis_of(w, p), ORDER[i]), device_id_type=MESH,
        )

    def copy3(w, p, i):
        axis = axis_of(w, p)
        return pltpu.make_async_remote_copy(
            src_ref=whole.at[w, p, at[axis]], dst_ref=whole.at[w, p, at[axis]],
            send_sem=send3.at[w, p, i], recv_sem=recv3.at[w, p, i], device_id=along(axis, ORDER[i]), device_id_type=MESH,
        )

    def first_on(w):
        return at[axis_of(w, 1)] == 0

    def extra1(w):
        axis = axis_of(w, 1)
        return pltpu.make_async_remote_copy(
            src_ref=extras.at[w], dst_ref=ext1.at[w, at[axis] - 1], send_sem=ext_send.at[w, 0],
            recv_sem=ext_recv1.at[w, at[axis] - 1], device_id=along(axis, 8 - at[axis]), device_id_type=MESH,
        )

    def extra1_here(w, i):
        return pltpu.make_async_remote_copy(
            src_ref=extras.at[w], dst_ref=ext1.at[w, i], send_sem=ext_send.at[w, 0],
            recv_sem=ext_recv1.at[w, i], device_id=along(axis_of(w, 1), 1), device_id_type=MESH,
        )

    def extra2(w, i):
        return pltpu.make_async_remote_copy(
            src_ref=ext_mine.at[w], dst_ref=ext2.at[w, i], send_sem=ext_send.at[w, 1 + i],
            recv_sem=ext_recv2.at[w, i], device_id=along(1 - axis_of(w, 1), ORDER[i]), device_id_type=MESH,
        )

    def extra3(w, i):
        return pltpu.make_async_remote_copy(
            src_ref=ext_all.at[w], dst_ref=ext_all.at[w], send_sem=ext_send.at[w, 8 + i],
            recv_sem=ext_recv3.at[w], device_id=along(axis_of(w, 1), ORDER[i]), device_id_type=MESH,
        )

    for copy in loads[:3]:
        copy.wait()
    sums = [row_sums(index_ref[w : w + 1, :], value_ref[w : w + 1, :], var_ref[w : w + 1, :]) for w in range(2)]
    for w in range(2):
        loads[3 + w].wait()
        k12, mixed, extra = pack(*local_sums(ens_ref[w], *sums[w]))
        parts[w, 0] = k12.reshape(8, SHARD, 128)
        parts[w, 1] = mixed.reshape(8, SHARD, 128)
        extras[w] = extra
    def send1(axis):
        for w in range(2):
            p = (axis + w) % 2
            for i in range(7):
                copy1(w, p, i).start()
            if p == 1:
                @pl.when(~first_on(w))
                def _():
                    extra1(w).start()

    pl.semaphore_wait(barrier, jnp.where(core == 0, 21, 15))
    pl.semaphore_signal(ready, inc=1, device_id=sibling, device_id_type=MESH)

    @pl.when(core == 0)
    def _():
        send1(0)
        pl.semaphore_wait(ready, 1)
        send1(1)

    @pl.when(core == 1)
    def _():
        send1(1)
        pl.semaphore_wait(ready, 1)
        send1(0)

    for w, p in blocks:
        total = parts[w, p, at[axis_of(w, p)]]
        for i in range(7):
            copy1(w, p, i).wait_recv()
            total = total + got1[w, p, i]
        mine[w, p] = total
        for i in range(7):
            copy2(w, p, i).start()
        if p == 1:
            @pl.when(first_on(w))
            def _():
                total = extras[w]
                for i in range(7):
                    extra1_here(w, i).wait_recv()
                    total = total + ext1[w, i]
                ext_mine[w] = total
                for i in range(7):
                    extra2(w, i).start()

    for w, p in blocks:
        total = mine[w, p]
        for i in range(7):
            copy2(w, p, i).wait_recv()
            total = total + got2[w, p, i]
        whole[w, p, at[axis_of(w, p)]] = total
        for i in range(7):
            copy3(w, p, i).start()
        if p == 1:
            @pl.when(first_on(w))
            def _():
                total = ext_mine[w]
                for i in range(7):
                    extra2(w, i).wait_recv()
                    total = total + ext2[w, i]
                ext_all[w] = total
                for i in range(7):
                    extra3(w, i).start()

    for w, p in blocks:
        for i in range(7):
            copy1(w, p, i).wait_send()
    begun = []
    for w in range(2):
        for p in range(2):
            for i in range(7):
                copy3(w, p, i).wait_recv()

        @pl.when(~first_on(w))
        def _():
            extra3(w, 0).wait_recv()

        begun.append(begin(*unpack(whole[w, 0].reshape(128, 128), whole[w, 1].reshape(128, 128), ext_all[w])))
    h0, h1 = transforms(begun)
    h0, h1 = split(h0), split(h1)

    def swap(n):
        rows = pl.ds(128 * n, 128)
        return pltpu.make_async_remote_copy(
            src_ref=pair.at[core, rows], dst_ref=pair.at[core, rows], send_sem=core_send.at[n], recv_sem=core_recv.at[n],
            device_id=sibling, device_id_type=MESH,
        )

    for n in range(2):
        rows = slice(128 * n, 128 * (n + 1))
        pair[core, rows] = dot3((h1[0][rows], h1[1][rows]), h0)
        swap(n).start()
    for w, p in blocks:
        for i in range(7):
            copy2(w, p, i).wait_send()
            copy3(w, p, i).wait_send()
    for w in range(2):
        @pl.when(first_on(w))
        def _():
            for i in range(7):
                extra2(w, i).wait_send()
                extra3(w, i).wait_send()

        @pl.when(~first_on(w))
        def _():
            extra1(w).wait_send()

    swap(0).wait_recv()

    @pl.when(core == 1)
    def _():
        swap(1).wait_recv()

    even = split(pair[0])

    def copy_x(by, n):
        rows = pl.ds(CHUNK * n, CHUNK)
        return pltpu.make_async_remote_copy(
            src_ref=half.at[rows], dst_ref=chips.at[x - 1, core, rows], send_sem=x_send.at[by - 1, n],
            recv_sem=x_recv.at[x - 1, n], device_id=on_x(-by), device_id_type=MESH,
        )

    def arrived(j, n):
        rows = pl.ds(CHUNK * n, CHUNK)
        return pltpu.make_async_remote_copy(
            src_ref=half.at[rows], dst_ref=chips.at[j, core, rows], send_sem=x_send.at[0, n],
            recv_sem=x_recv.at[j, n], device_id=sibling, device_id_type=MESH,
        )

    def pass_on(j, n):
        rows = pl.ds(CHUNK * n, CHUNK)
        return pltpu.make_async_remote_copy(
            src_ref=chips.at[j, core, rows], dst_ref=chips.at[j, core, rows], send_sem=f_send.at[j, n],
            recv_sem=f_recv.at[j, n], device_id=sibling, device_id_type=MESH,
        )

    def passed(j, n):
        rows = pl.ds(CHUNK * n, CHUNK)
        return pltpu.make_async_remote_copy(
            src_ref=chips.at[j, core, rows], dst_ref=chips.at[j, 1 - core, rows], send_sem=f_send.at[j, n],
            recv_sem=f_recv.at[j, n], device_id=sibling, device_id_type=MESH,
        )

    def relay(n):
        rows = pl.ds(CHUNK * n, CHUNK)
        return pltpu.make_async_remote_copy(
            src_ref=chips.at[2 - x, core, rows], dst_ref=chips.at[2 - x, core, rows], send_sem=relay_send.at[n],
            recv_sem=x_recv.at[2 - x, n], device_id={"tm": (1 - x) * 2 + core, "space": s}, device_id_type=MESH,
        )

    for n in range(CHUNKS):
        top = pl.multiple_of(core * 128 + CHUNK * n, CHUNK)
        half[CHUNK * n : CHUNK * (n + 1), :] = dot3(split(pair[1, pl.ds(top, CHUNK), :]), even)
        for by in (2, 3, 1) if n >= RELAYED else (3, 1):
            @pl.when(x >= by)
            def _():
                copy_x(by, n).start()

    @pl.when(core == 0)
    def _():
        swap(1).wait_recv()
        odd = split(pair[1])
        tail[:, :M] = dot3(odd, even)
        tail[:, M:] = dot3(odd, h1)

    @pl.when(core == 1)
    def _():
        tail[:, :M] = pair[1]
        tail[:, M:] = h1[0].astype(F32) + h1[1].astype(F32)

    def receive(by, n):
        @pl.when(x + by <= 3)
        def _():
            arrived(x + by - 1, n).wait_recv()
            pass_on(x + by - 1, n).start()

    for n in range(CHUNKS):
        receive(1, n)
        receive(3, n)
        if n < RELAYED:
            @pl.when(x <= 1)
            def _():
                relay(n).start()
        else:
            receive(2, n)
    for n in range(RELAYED):
        receive(2, n)

    def chip(j):
        for n in range(CHUNKS):
            passed(j, n).wait_recv()
        return split(chips[j].reshape(M, M))

    @pl.when(x == 0)
    def _():
        tail[...] = dot3(chip(0), split(tail[...]))

    @pl.when(x <= 1)
    def _():
        first = chip(1)

        @pl.when(x == 0)
        def _():
            last[...] = dot3(chip(2), first)

        @pl.when(x == 1)
        def _():
            tail[...] = dot3(first, split(tail[...]))

    @pl.when((x == 1) | (x == 2))
    def _():
        for n in range(CHUNKS):
            passed(2, n).wait_recv()
        last[...] = chips[2].reshape(M, M)

    @pl.when(x <= 2)
    def _():
        tail[...] = dot3(split(last[...]), split(tail[...]))

    out_ref[0] = tail[:, :M].astype(BF16)
    out_ref[1] = tail[:, M:].astype(BF16)

    @pl.when(x <= 1)
    def _():
        for n in range(RELAYED):
            relay(n).wait_send()

    for n in range(2):
        swap(n).wait_send()
    for n in range(CHUNKS):
        for by in (1, 2, 3) if n >= RELAYED else (1, 3):
            @pl.when(x >= by)
            def _():
                copy_x(by, n).wait_send()
        for j in range(3):
            @pl.when(x <= j)
            def _():
                pass_on(j, n).wait_send()


def smooth_kernel(ens_ref, suffix_ref, out_ref, held, sem):
    steps = held.shape[0]
    rows = held.shape[1]
    each = steps // 2

    def copy(i):
        return pltpu.make_async_copy(held.at[i], out_ref.at[i // each, pl.ds((i % each) * rows, rows)], sem.at[i])

    for i in range(steps):
        block = ens_ref[i // each, (i % each) * rows : (i % each + 1) * rows, :]
        held[i] = dot_nt(block, suffix_ref[i // each]).astype(BF16)
        copy(i).start()
    for i in range(steps):
        copy(i).wait()


def on_device(ensemble, obs_index, obs_value, obs_var):
    vmem = pl.BlockSpec(memory_space=pltpu.VMEM)
    sems = pltpu.SemaphoreType.DMA
    small = [pltpu.VMEM(a.shape, a.dtype) for a in (obs_index, obs_value, obs_var)]
    suffix, held = pl.pallas_call(
        suffix_kernel,
        out_shape=(jax.ShapeDtypeStruct((2, M, M), BF16), jax.ShapeDtypeStruct(ensemble.shape, BF16)),
        in_specs=[pl.BlockSpec(memory_space=pltpu.HBM)] * 4,
        out_specs=(vmem, vmem),
        scratch_shapes=small + [
            sems((5,)),
            pltpu.VMEM((2, 2, 8, SHARD, 128), F32),
            pltpu.VMEM((2, 2, 7, SHARD, 128), F32),
            pltpu.VMEM((2, 2, SHARD, 128), F32),
            pltpu.VMEM((2, 2, 7, SHARD, 128), F32),
            pltpu.VMEM((2, 2, 8, SHARD, 128), F32),
            pltpu.VMEM((2, 8, 128), F32),
            pltpu.VMEM((2, M, M), F32),
            pltpu.VMEM((128, M), F32),
            pltpu.VMEM((3, 2, 128, M), F32),
            pltpu.VMEM((M, 2 * M), F32),
            sems((2, 2, 7)), sems((2, 2, 7)), sems((2, 2, 7)), sems((2, 2, 7)), sems((2, 2, 7)), sems((2, 2, 7)),
            sems((2,)), sems((2,)), sems((3, CHUNKS)), sems((3, CHUNKS)), sems((3, CHUNKS)), sems((3, CHUNKS)),
            pltpu.VMEM((M, M), F32), sems((RELAYED,)),
            pltpu.VMEM((2, 7, 8, 128), F32), pltpu.VMEM((2, 8, 128), F32),
            pltpu.VMEM((2, 7, 8, 128), F32), pltpu.VMEM((2, 8, 128), F32),
            sems((2, 15)), sems((2, 7)), sems((2, 7)), sems((2,)), pltpu.SemaphoreType.REGULAR,
        ],
        compiler_params=pltpu.CompilerParams(collective_id=0, has_side_effects=True, vmem_limit_bytes=VMEM_LIMIT),
        name="suffixes",
    )(*(pltpu.with_memory_space_constraint(a, pltpu.HBM) for a in (ensemble, obs_index, obs_value, obs_var)))
    return pl.pallas_call(
        smooth_kernel,
        out_shape=jax.ShapeDtypeStruct(ensemble.shape, BF16),
        in_specs=[vmem] * 2,
        out_specs=pl.BlockSpec(memory_space=pltpu.HBM),
        scratch_shapes=[pltpu.VMEM((8, ensemble.shape[1] // 4, M), BF16), sems((8,))],
        compiler_params=pltpu.CompilerParams(vmem_limit_bytes=VMEM_LIMIT),
        name="smooth",
    )(held, suffix)


def solution(mesh):
    placed = (P("tm", "space", None), P("tm", "space"), P("tm", "space"), P("tm", "space"))
    return jax.shard_map(
        on_device, mesh=mesh, in_specs=placed, out_specs=P("tm", "space", None), check_vma=False
    )
```

```python
import jax
import jax.numpy as jnp
from jax import lax
from jax.experimental import pallas as pl
from jax.experimental.pallas import tpu as pltpu
from jax.sharding import PartitionSpec as P

NS_ITERS = 6
M = 256
MESH = pl.DeviceIdType.MESH
F32 = jnp.float32
BF16 = jnp.bfloat16
ORDER = (4, 3, 5, 2, 6, 1, 7)
SHARD = 16
CHUNK = 32
CHUNKS = 128 // CHUNK
RELAYED = 2
VMEM_LIMIT = 20 * 2**20


def dot(a, b):
    return jnp.dot(a, b, preferred_element_type=F32)


def dot_nt(a, b):
    return lax.dot_general(a, b, (((1,), (1,)), ((), ())), preferred_element_type=F32)


def split(a):
    high = a.astype(BF16)
    return high, (a - high.astype(F32)).astype(BF16)


def dot3(a, b):
    left = jnp.concatenate([a[0], a[1], a[0]], axis=1)
    right = jnp.concatenate([b[0], b[0], b[1]], axis=0)
    return dot(left, right)


def row_sums(index, value, var):
    inv = 1.0 / var
    low = index & 127
    high = index >> 7
    count = index.shape[1]
    at_low = jnp.where(lax.broadcasted_iota(jnp.int32, (128, count), 0) == low, 1.0, 0.0).astype(BF16)
    at_high = lax.broadcasted_iota(jnp.int32, (16, count), 0) == high
    terms = jnp.concatenate([jnp.where(at_high, inv, 0.0), jnp.where(at_high, value * inv, 0.0)], axis=0)
    first = terms.astype(BF16)
    rest = terms - first.astype(F32)
    second = rest.astype(BF16)
    third = (rest - second.astype(F32)).astype(BF16)
    rows = dot_nt(jnp.concatenate([first, second, third], axis=1), jnp.concatenate([at_low] * 3, axis=1))
    w_row = jnp.concatenate([rows[i : i + 1, :] for i in range(16)], axis=1)
    s_row = jnp.concatenate([rows[16 + i : 17 + i, :] for i in range(16)], axis=1)
    s_first, s_second = split(s_row)
    return w_row, jnp.concatenate([s_first, s_second, jnp.zeros((14, s_row.shape[1]), BF16)], axis=0)


def local_sums(ens, w_row, s_both):
    first, second = split(ens.T.astype(F32) * w_row)
    proj = dot(s_both, ens)
    return dot(first, ens) + dot(second, ens), proj[0:1, :] + proj[1:2, :]


def pack(gram, proj):
    r = lax.broadcasted_iota(jnp.int32, (128, 128), 0)
    c = lax.broadcasted_iota(jnp.int32, (128, 128), 1)
    k11, k12, k22 = gram[:128, :128], gram[:128, 128:], gram[128:, 128:]
    mixed = jnp.where(r >= c, k11, k22)
    diag = jnp.sum(jnp.where(r == c, k22, 0.0), axis=0, keepdims=True)
    extra = jnp.concatenate([diag, proj[:, :128], proj[:, 128:], jnp.zeros((5, 128), F32)], axis=0)
    return k12, mixed, extra


def unpack(k12, mixed, extra):
    r = lax.broadcasted_iota(jnp.int32, (128, 128), 0)
    c = lax.broadcasted_iota(jnp.int32, (128, 128), 1)
    turned = mixed.T
    k11 = jnp.where(r >= c, mixed, turned)
    k22 = jnp.where(r < c, mixed, jnp.where(r == c, extra[0:1, :], turned))
    gram = jnp.concatenate(
        [jnp.concatenate([k11, k12], axis=1), jnp.concatenate([k12.T, k22], axis=1)], axis=0
    )
    return gram, jnp.concatenate([extra[1:2, :], extra[2:3, :]], axis=1)


def identity():
    r = lax.broadcasted_iota(jnp.int32, (M, M), 0)
    c = lax.broadcasted_iota(jnp.int32, (M, M), 1)
    return jnp.where(r == c, 1.0, 0.0).astype(F32)


def begin(gram, proj):
    eye = identity()
    col_mean = jnp.mean(gram, axis=0, keepdims=True)
    row_mean = jnp.mean(gram, axis=1, keepdims=True)
    amat = gram - row_mean - (col_mean - jnp.mean(col_mean, axis=1, keepdims=True)) + (M - 1.0) * eye
    scale = jnp.sqrt(jnp.sum(jnp.sum(amat * amat, axis=0, keepdims=True), axis=1, keepdims=True))
    start = amat * (1.0 / scale)
    proj = proj - col_mean
    proj = proj - jnp.mean(proj, axis=1, keepdims=True)
    b = (0.5 * start).astype(BF16)
    return scale, proj, 1.5 * start - dot(start.astype(BF16), b), 1.5 * eye - b.astype(F32), b


def transforms(begun):
    eye = identity()
    count = range(len(begun))
    scales, projs, y, z, before = (list(a) for a in zip(*begun))

    def twice(a, b):
        return dot(jnp.concatenate([a, a], axis=1), jnp.concatenate(b, axis=0))

    def after(a, b):
        return dot(jnp.concatenate(a, axis=1), jnp.concatenate([b, b], axis=0))

    b = [(0.5 * dot(z[w].astype(BF16), y[w].astype(BF16))).astype(BF16) for w in count]
    z = [1.5 * z[w] - (1.5 * b[w].astype(F32) - dot(b[w], before[w])) for w in count]
    y = [1.5 * y[w] - dot(y[w].astype(BF16), b[w]) for w in count]
    for step in range(2, NS_ITERS - 1):
        zs, ys = [split(a) for a in z], [split(a) for a in y]
        b = [(0.5 * dot(zs[w][0], ys[w][0])).astype(BF16) for w in count]
        z = [1.5 * z[w] - twice(b[w], zs[w]) for w in count]
        y = [1.5 * y[w] - after(ys[w], b[w]) for w in count]
    zs, ys = [split(a) for a in z], [split(a) for a in y]
    t = [split(1.5 * eye - 0.5 * dot3(zs[w], ys[w])) for w in count]
    z = [dot3(t[w], zs[w]) for w in count]
    turned = []
    for w in count:
        both = split(z[w])
        vec = dot3(split(jnp.broadcast_to(projs[w], (16, M))), both)
        wmean = dot3(split(vec), both)[0:1, :] / scales[w]
        wmean = wmean - jnp.mean(wmean, axis=1, keepdims=True)
        wtrans = z[w] * (jnp.sqrt(M - 1.0) / jnp.sqrt(scales[w]))
        turned.append(wtrans - jnp.mean(wtrans, axis=1, keepdims=True) + (wmean + 1.0 / M))
    return turned


def suffix_kernel(
    ens_in, index_in, value_in, var_in, out_ref, ens_ref,
    index_ref, value_ref, var_ref, load, parts, got1, mine, got2, whole, extras, pair, half, chips, tail,
    send_1, recv1, send2, recv2, send3, recv3, core_send, core_recv, x_send, x_recv, f_send, f_recv, relay_send,
    ext1, ext_mine, ext2, ext_all, ext_send, ext_recv1, ext_recv2, ext_recv3, ready,
):
    t = lax.axis_index("tm")
    s = lax.axis_index("space")
    x, core = t // 2, t % 2
    at = (s // 8, s % 8)

    def along(axis, by):
        spot = list(at)
        spot[axis] = (at[axis] + by) % 8
        return {"tm": t, "space": spot[0] * 8 + spot[1]}

    def on_x(by):
        return {"tm": ((x + by + 4) % 4) * 2 + core, "space": s}

    sibling = {"tm": x * 2 + 1 - core, "space": s}

    pairs = ((index_in, index_ref), (value_in, value_ref), (var_in, var_ref))
    loads = [pltpu.make_async_copy(a, b, load.at[i]) for i, (a, b) in enumerate(pairs)]
    loads += [pltpu.make_async_copy(ens_in.at[w], ens_ref.at[w], load.at[3 + w]) for w in range(2)]
    for copy in loads:
        copy.start()

    barrier = pltpu.get_barrier_semaphore()
    for by in ORDER:
        for axis in range(2):
            there = {"tm": x * 2 + axis, "space": along(axis, by)["space"]}
            pl.semaphore_signal(barrier, inc=1, device_id=there, device_id_type=MESH)
    for by in (1, 2, 3):
        there = {"tm": ((x + by) % 4) * 2, "space": s}
        pl.semaphore_signal(barrier, inc=1, device_id=there, device_id_type=MESH)
    pl.semaphore_signal(barrier, inc=1, device_id=sibling, device_id_type=MESH)

    blocks = [(w, p) for w in range(2) for p in range(2)]

    def axis_of(w, p):
        return (w + p) % 2

    def copy1(w, p, i):
        axis, by = axis_of(w, p), ORDER[i]
        return pltpu.make_async_remote_copy(
            src_ref=parts.at[w, p, (at[axis] + by) % 8], dst_ref=got1.at[w, p, i],
            send_sem=send_1.at[w, p, i], recv_sem=recv1.at[w, p, i], device_id=along(axis, by), device_id_type=MESH,
        )

    def copy2(w, p, i):
        return pltpu.make_async_remote_copy(
            src_ref=mine.at[w, p], dst_ref=got2.at[w, p, i],
            send_sem=send2.at[w, p, i], recv_sem=recv2.at[w, p, i],
            device_id=along(1 - axis_of(w, p), ORDER[i]), device_id_type=MESH,
        )

    def copy3(w, p, i):
        axis = axis_of(w, p)
        return pltpu.make_async_remote_copy(
            src_ref=whole.at[w, p, at[axis]], dst_ref=whole.at[w, p, at[axis]],
            send_sem=send3.at[w, p, i], recv_sem=recv3.at[w, p, i], device_id=along(axis, ORDER[i]), device_id_type=MESH,
        )

    def first_on(w):
        return at[axis_of(w, 1)] == 0

    def extra1(w):
        axis = axis_of(w, 1)
        return pltpu.make_async_remote_copy(
            src_ref=extras.at[w], dst_ref=ext1.at[w, at[axis] - 1], send_sem=ext_send.at[w, 0],
            recv_sem=ext_recv1.at[w, at[axis] - 1], device_id=along(axis, 8 - at[axis]), device_id_type=MESH,
        )

    def extra1_here(w, i):
        return pltpu.make_async_remote_copy(
            src_ref=extras.at[w], dst_ref=ext1.at[w, i], send_sem=ext_send.at[w, 0],
            recv_sem=ext_recv1.at[w, i], device_id=along(axis_of(w, 1), 1), device_id_type=MESH,
        )

    def extra2(w, i):
        return pltpu.make_async_remote_copy(
            src_ref=ext_mine.at[w], dst_ref=ext2.at[w, i], send_sem=ext_send.at[w, 1 + i],
            recv_sem=ext_recv2.at[w, i], device_id=along(1 - axis_of(w, 1), ORDER[i]), device_id_type=MESH,
        )

    def extra3(w, i):
        return pltpu.make_async_remote_copy(
            src_ref=ext_all.at[w], dst_ref=ext_all.at[w], send_sem=ext_send.at[w, 8 + i],
            recv_sem=ext_recv3.at[w], device_id=along(axis_of(w, 1), ORDER[i]), device_id_type=MESH,
        )

    for copy in loads[:3]:
        copy.wait()
    sums = [row_sums(index_ref[w : w + 1, :], value_ref[w : w + 1, :], var_ref[w : w + 1, :]) for w in range(2)]
    for w in range(2):
        loads[3 + w].wait()
        k12, mixed, extra = pack(*local_sums(ens_ref[w], *sums[w]))
        parts[w, 0] = k12.reshape(8, SHARD, 128)
        parts[w, 1] = mixed.reshape(8, SHARD, 128)
        extras[w] = extra
    def send1(axis):
        for w in range(2):
            p = (axis + w) % 2
            for i in range(7):
                copy1(w, p, i).start()
            if p == 1:
                @pl.when(~first_on(w))
                def _():
                    extra1(w).start()

    pl.semaphore_wait(barrier, jnp.where(core == 0, 21, 15))
    pl.semaphore_signal(ready, inc=1, device_id=sibling, device_id_type=MESH)

    @pl.when(core == 0)
    def _():
        send1(0)
        pl.semaphore_wait(ready, 1)
        send1(1)

    @pl.when(core == 1)
    def _():
        send1(1)
        pl.semaphore_wait(ready, 1)
        send1(0)

    for w, p in blocks:
        total = parts[w, p, at[axis_of(w, p)]]
        for i in range(7):
            copy1(w, p, i).wait_recv()
            total = total + got1[w, p, i]
        mine[w, p] = total
        for i in range(7):
            copy2(w, p, i).start()
        if p == 1:
            @pl.when(first_on(w))
            def _():
                total = extras[w]
                for i in range(7):
                    extra1_here(w, i).wait_recv()
                    total = total + ext1[w, i]
                ext_mine[w] = total
                for i in range(7):
                    extra2(w, i).start()

    for w, p in blocks:
        total = mine[w, p]
        for i in range(7):
            copy2(w, p, i).wait_recv()
            total = total + got2[w, p, i]
        whole[w, p, at[axis_of(w, p)]] = total
        for i in range(7):
            copy3(w, p, i).start()
        if p == 1:
            @pl.when(first_on(w))
            def _():
                total = ext_mine[w]
                for i in range(7):
                    extra2(w, i).wait_recv()
                    total = total + ext2[w, i]
                ext_all[w] = total
                for i in range(7):
                    extra3(w, i).start()

    for w, p in blocks:
        for i in range(7):
            copy1(w, p, i).wait_send()
    begun = []
    for w in range(2):
        for p in range(2):
            for i in range(7):
                copy3(w, p, i).wait_recv()

        @pl.when(~first_on(w))
        def _():
            extra3(w, 0).wait_recv()

        begun.append(begin(*unpack(whole[w, 0].reshape(128, 128), whole[w, 1].reshape(128, 128), ext_all[w])))
    h0, h1 = transforms(begun)
    h0, h1 = split(h0), split(h1)

    def swap(n):
        rows = pl.ds(128 * n, 128)
        return pltpu.make_async_remote_copy(
            src_ref=pair.at[core, rows], dst_ref=pair.at[core, rows], send_sem=core_send.at[n], recv_sem=core_recv.at[n],
            device_id=sibling, device_id_type=MESH,
        )

    for n in range(2):
        rows = slice(128 * n, 128 * (n + 1))
        pair[core, rows] = dot3((h1[0][rows], h1[1][rows]), h0)
        swap(n).start()
    for w, p in blocks:
        for i in range(7):
            copy2(w, p, i).wait_send()
            copy3(w, p, i).wait_send()
    for w in range(2):
        @pl.when(first_on(w))
        def _():
            for i in range(7):
                extra2(w, i).wait_send()
                extra3(w, i).wait_send()

        @pl.when(~first_on(w))
        def _():
            extra1(w).wait_send()

    swap(0).wait_recv()

    @pl.when(core == 1)
    def _():
        swap(1).wait_recv()

    even = split(pair[0])

    def copy_x(by, n):
        rows = pl.ds(CHUNK * n, CHUNK)
        return pltpu.make_async_remote_copy(
            src_ref=half.at[rows], dst_ref=chips.at[x - 1, core, rows], send_sem=x_send.at[by - 1, n],
            recv_sem=x_recv.at[x - 1, n], device_id=on_x(-by), device_id_type=MESH,
        )

    def arrived(j, n):
        rows = pl.ds(CHUNK * n, CHUNK)
        return pltpu.make_async_remote_copy(
            src_ref=half.at[rows], dst_ref=chips.at[j, core, rows], send_sem=x_send.at[0, n],
            recv_sem=x_recv.at[j, n], device_id=sibling, device_id_type=MESH,
        )

    def pass_on(j, n):
        rows = pl.ds(CHUNK * n, CHUNK)
        return pltpu.make_async_remote_copy(
            src_ref=chips.at[j, core, rows], dst_ref=chips.at[j, core, rows], send_sem=f_send.at[j, n],
            recv_sem=f_recv.at[j, n], device_id=sibling, device_id_type=MESH,
        )

    def passed(j, n):
        rows = pl.ds(CHUNK * n, CHUNK)
        return pltpu.make_async_remote_copy(
            src_ref=chips.at[j, core, rows], dst_ref=chips.at[j, 1 - core, rows], send_sem=f_send.at[j, n],
            recv_sem=f_recv.at[j, n], device_id=sibling, device_id_type=MESH,
        )

    def relay(n):
        rows = pl.ds(CHUNK * n, CHUNK)
        return pltpu.make_async_remote_copy(
            src_ref=chips.at[2 - x, core, rows], dst_ref=chips.at[2 - x, core, rows], send_sem=relay_send.at[n],
            recv_sem=x_recv.at[2 - x, n], device_id={"tm": (1 - x) * 2 + core, "space": s}, device_id_type=MESH,
        )

    for n in range(CHUNKS):
        top = pl.multiple_of(core * 128 + CHUNK * n, CHUNK)
        half[CHUNK * n : CHUNK * (n + 1), :] = dot3(split(pair[1, pl.ds(top, CHUNK), :]), even)
        for by in (2, 3, 1) if n >= RELAYED else (3, 1):
            @pl.when(x >= by)
            def _():
                copy_x(by, n).start()

    @pl.when(core == 0)
    def _():
        swap(1).wait_recv()
        odd = split(pair[1])
        tail[:, :M] = dot3(odd, even)
        tail[:, M:] = dot3(odd, h1)

    @pl.when(core == 1)
    def _():
        tail[:, :M] = pair[1]
        tail[:, M:] = h1[0].astype(F32) + h1[1].astype(F32)

    def receive(by, n):
        @pl.when(x + by <= 3)
        def _():
            arrived(x + by - 1, n).wait_recv()
            pass_on(x + by - 1, n).start()

    for n in range(CHUNKS):
        receive(1, n)
        receive(3, n)
        if n < RELAYED:
            @pl.when(x <= 1)
            def _():
                relay(n).start()
        else:
            receive(2, n)
    for n in range(RELAYED):
        receive(2, n)

    def whole_chip(j):
        for n in range(CHUNKS):
            passed(j, n).wait_recv()
        tail[...] = dot3(split(chips[j].reshape(M, M)), split(tail[...]))

    def by_chunks(j):
        right = split(tail[...])
        for n in [*range(RELAYED, CHUNKS), *range(RELAYED)]:
            passed(j, n).wait_recv()
            rows = slice(CHUNK * n, CHUNK * (n + 1))
            done = dot3(split(chips[j, :, rows].reshape(2 * CHUNK, M)), right)
            for h in range(2):
                tail[128 * h + CHUNK * n : 128 * h + CHUNK * (n + 1)] = done[CHUNK * h : CHUNK * (h + 1)]

    @pl.when(x == 0)
    def _():
        whole_chip(0)
        by_chunks(1)
        whole_chip(2)

    @pl.when(x == 1)
    def _():
        whole_chip(1)

    @pl.when((x == 1) | (x == 2))
    def _():
        by_chunks(2)

    out_ref[0] = tail[:, :M].astype(BF16)
    out_ref[1] = tail[:, M:].astype(BF16)

    @pl.when(x <= 1)
    def _():
        for n in range(RELAYED):
            relay(n).wait_send()

    for n in range(2):
        swap(n).wait_send()
    for n in range(CHUNKS):
        for by in (1, 2, 3) if n >= RELAYED else (1, 3):
            @pl.when(x >= by)
            def _():
                copy_x(by, n).wait_send()
        for j in range(3):
            @pl.when(x <= j)
            def _():
                pass_on(j, n).wait_send()


def smooth_kernel(ens_ref, suffix_ref, out_ref, held, sem):
    steps = held.shape[0]
    rows = held.shape[1]
    each = steps // 2

    def copy(i):
        return pltpu.make_async_copy(held.at[i], out_ref.at[i // each, pl.ds((i % each) * rows, rows)], sem.at[i])

    for i in range(steps):
        block = ens_ref[i // each, (i % each) * rows : (i % each + 1) * rows, :]
        held[i] = dot_nt(block, suffix_ref[i // each]).astype(BF16)
        copy(i).start()
    for i in range(steps):
        copy(i).wait()


def on_device(ensemble, obs_index, obs_value, obs_var):
    vmem = pl.BlockSpec(memory_space=pltpu.VMEM)
    sems = pltpu.SemaphoreType.DMA
    small = [pltpu.VMEM(a.shape, a.dtype) for a in (obs_index, obs_value, obs_var)]
    suffix, held = pl.pallas_call(
        suffix_kernel,
        out_shape=(jax.ShapeDtypeStruct((2, M, M), BF16), jax.ShapeDtypeStruct(ensemble.shape, BF16)),
        in_specs=[pl.BlockSpec(memory_space=pltpu.HBM)] * 4,
        out_specs=(vmem, vmem),
        scratch_shapes=small + [
            sems((5,)),
            pltpu.VMEM((2, 2, 8, SHARD, 128), F32),
            pltpu.VMEM((2, 2, 7, SHARD, 128), F32),
            pltpu.VMEM((2, 2, SHARD, 128), F32),
            pltpu.VMEM((2, 2, 7, SHARD, 128), F32),
            pltpu.VMEM((2, 2, 8, SHARD, 128), F32),
            pltpu.VMEM((2, 8, 128), F32),
            pltpu.VMEM((2, M, M), F32),
            pltpu.VMEM((128, M), F32),
            pltpu.VMEM((3, 2, 128, M), F32),
            pltpu.VMEM((M, 2 * M), F32),
            sems((2, 2, 7)), sems((2, 2, 7)), sems((2, 2, 7)), sems((2, 2, 7)), sems((2, 2, 7)), sems((2, 2, 7)),
            sems((2,)), sems((2,)), sems((3, CHUNKS)), sems((3, CHUNKS)), sems((3, CHUNKS)), sems((3, CHUNKS)),
            sems((RELAYED,)),
            pltpu.VMEM((2, 7, 8, 128), F32), pltpu.VMEM((2, 8, 128), F32),
            pltpu.VMEM((2, 7, 8, 128), F32), pltpu.VMEM((2, 8, 128), F32),
            sems((2, 15)), sems((2, 7)), sems((2, 7)), sems((2,)), pltpu.SemaphoreType.REGULAR,
        ],
        compiler_params=pltpu.CompilerParams(collective_id=0, has_side_effects=True, vmem_limit_bytes=VMEM_LIMIT),
        name="suffixes",
    )(*(pltpu.with_memory_space_constraint(a, pltpu.HBM) for a in (ensemble, obs_index, obs_value, obs_var)))
    return pl.pallas_call(
        smooth_kernel,
        out_shape=jax.ShapeDtypeStruct(ensemble.shape, BF16),
        in_specs=[vmem] * 2,
        out_specs=pl.BlockSpec(memory_space=pltpu.HBM),
        scratch_shapes=[pltpu.VMEM((8, ensemble.shape[1] // 4, M), BF16), sems((8,))],
        compiler_params=pltpu.CompilerParams(vmem_limit_bytes=VMEM_LIMIT),
        name="smooth",
    )(held, suffix)


def solution(mesh):
    placed = (P("tm", "space", None), P("tm", "space"), P("tm", "space"), P("tm", "space"))
    return jax.shard_map(
        on_device, mesh=mesh, in_specs=placed, out_specs=P("tm", "space", None), check_vma=False
    )
```
